32 devices in a mesh: seq: 8 (over z, x), head: 4 (over y, core).
Axes of the slice: x: 2, y: 2, z: 4, core: 2. Of those that a mesh axis runs over, the one named last changes fastest.
Arguments:
- tokens: bfloat16 [4096, 4096], P('seq', 'head'), may hold values from -6 to 6
- norm_gain: float32 [4096], replicated, may hold values from 0.1 to 1.9
- w_query: bfloat16 [4096, 4096], P(None, 'head')
- key_weight: bfloat16 [4096, 1024], P(None, 'head')
- value_weight: bfloat16 [4096, 1024], P(None, 'head'), may hold values from -0.09375 to 0.09375
- w_out: bfloat16 [4096, 4096], P('head'), may hold values from -0.5 to 0.5
- ancestor_blocks: int32 [32, 8], P('seq'), may hold values from -1 to 30, as said below
- visible_counts: int32 [32, 8], P('seq'), may hold values from 0 to 128, as said below
Outputs:
- sublayer_out: bfloat16 [4096, 4096], P('seq', 'head')
The draws below stay inside these ranges and needn't reach their ends.
Inputs may be any that keep to these rules, and one draw needn't show every extreme that they name: `ancestor_blocks`: entry j of row b is block b's ancestor at depth j (the root block first), an earlier block; entries at and past block b's depth are -1. An ancestor that lies in another index of seq's tokens than block b is always the first block of that index's 512 tokens. The last block's parent is the block before it, whose parent is block 0. `visible_counts`: positive exactly where ancestor_blocks names a block, 0 elsewhere; the last block sees its parent whole.
All inputs are finite; a program needn't handle non-finite values.
Results may differ from the reference program's by a relative error of at most 0.019.
Values may be sent and summed in bfloat16 or wider, within the bound.
A program may use at most 64 MiB of HBM per device.

```python
import jax
import jax.numpy as jnp
from jax import lax

MODEL_WIDTH = 4096
QUERY_HEADS = 32
KEY_VALUE_HEADS = 8
HEAD_SIZE = 128
BLOCK_TOKENS = 128
DEPTH = 8
TOK_DEV = 512
TOKENS = 4096
N_HEAD = 4


def tree_tables(key):
    block_total = TOKENS // BLOCK_TOKENS
    per_device = TOK_DEV // BLOCK_TOKENS
    device_count = TOKENS // TOK_DEV
    chain_devices = min(DEPTH, device_count - 1)
    follow_key, score_key, cut_key = jax.random.split(key, 3)
    follow = jax.random.randint(follow_key, (block_total,), 0, 2)
    ranking = jax.random.randint(score_key, (block_total, block_total), 0, 1 << 20)
    cuts = jax.random.randint(cut_key, (block_total,), 1, BLOCK_TOKENS + 1)
    index_row = jnp.arange(block_total, dtype=jnp.int32)
    slot_row = jnp.arange(DEPTH, dtype=jnp.int32)

    def grow(carry, block_id):
        depths, lists, seen = carry
        device_id = block_id // per_device
        leading = block_id % per_device == 0
        before_ok = depths[block_id - 1] < DEPTH
        special = block_id == block_total - 2
        final = block_id == block_total - 1
        forced_lead = leading & (device_id <= chain_devices) & jnp.logical_not(special)
        forced_local = jnp.logical_not(leading) & (device_id <= chain_devices) & before_ok
        follow_local = jnp.logical_not(leading) & (follow[block_id] == 1) & before_ok
        chained = (forced_local | follow_local | final) & jnp.logical_not(special)
        reachable = (index_row // per_device == device_id) | (index_row % per_device == 0)
        allowed = (index_row < block_id) & (depths < DEPTH) & reachable
        ranked = jnp.where(allowed, ranking[block_id] * block_total + index_row, -1)
        chosen = jnp.argmax(ranked).astype(jnp.int32)
        parent = jnp.where(special, 0, jnp.where(forced_lead, block_id - per_device, jnp.where(chained, block_id - 1, chosen))).astype(jnp.int32)
        cut_len = jnp.where(chained | forced_lead, BLOCK_TOKENS, cuts[block_id]).astype(jnp.int32)
        level = depths[parent]
        new_list = jnp.where(slot_row == level, parent, lists[parent]).astype(jnp.int32)
        new_seen = jnp.where(slot_row == level, cut_len, seen[parent]).astype(jnp.int32)
        depths = depths.at[block_id].set(level + 1)
        lists = lists.at[block_id].set(new_list)
        seen = seen.at[block_id].set(new_seen)
        return ((depths, lists, seen), None)
    start = (jnp.zeros((block_total,), jnp.int32), jnp.full((block_total, DEPTH), -1, jnp.int32), jnp.zeros((block_total, DEPTH), jnp.int32))
    finals, unused = lax.scan(grow, start, jnp.arange(1, block_total, dtype=jnp.int32))
    return (finals[1], finals[2])


def draw_ancestor_blocks(key, part):
    return tree_tables(jax.random.fold_in(key, 7))[0]


def draw_visible_counts(key, part):
    return tree_tables(jax.random.fold_in(key, 7))[1]


def key_table(key):
    return jax.random.normal(key, (MODEL_WIDTH, KEY_VALUE_HEADS * HEAD_SIZE), jnp.float32) * MODEL_WIDTH ** (-0.5)


def draw_key_weight(key, part):
    return key_table(jax.random.fold_in(key, 11)).astype(jnp.bfloat16)


def draw_w_query(key, part):
    base = jax.random.normal(jax.random.fold_in(key, 13), (MODEL_WIDTH, QUERY_HEADS * HEAD_SIZE), jnp.float32) * MODEL_WIDTH ** (-0.5)
    return base.astype(jnp.bfloat16)


def shard_levels(key, extent, pieces, least, top_value):
    loudness, own = 1.0, jax.random.fold_in(key, 6)
    for position, blocks in pieces:
        draws = jnp.exp(jax.random.uniform(jax.random.fold_in(own, position), (blocks,), jnp.float32, least / len(pieces), top_value / len(pieces)))
        loudness = loudness * jnp.repeat(draws, extent[position] // blocks).reshape([-1 if axis == position else 1 for axis in range(len(extent))])
    return loudness


def normal_values(stream_key, shape, scale, limit, shards=(), kind=jnp.bfloat16):
    values = jax.random.normal(stream_key, shape, jnp.float32) * scale
    if len(shards) > 0:
        values = shard_levels(stream_key, shape, shards, -0.22, 0.18) * values
    return jnp.clip(values, min=-limit, max=limit).astype(kind)


def setup_inputs(seed: int = 0) -> dict:
    key_list = jax.random.split(jax.random.key(seed), 9)
    tokens = normal_values(key_list[0], (TOKENS, MODEL_WIDTH), 1.0, 6.0, ((0, 8), (1, 4)))
    norm_gain = jnp.clip(1.0 + 0.18 * jax.random.normal(key_list[1], (MODEL_WIDTH,), jnp.float32), 0.1, 1.9)
    w_query = draw_w_query(jax.random.fold_in(key_list[8], 71), 0)
    key_weight = draw_key_weight(jax.random.fold_in(key_list[8], 71), 0)
    value_weight = normal_values(key_list[4], (MODEL_WIDTH, KEY_VALUE_HEADS * HEAD_SIZE), MODEL_WIDTH ** -0.5, 0.09375, ((1, 4),))
    w_out = normal_values(key_list[5], (QUERY_HEADS * HEAD_SIZE, MODEL_WIDTH), HEAD_SIZE ** -0.5, 0.5, ((0, 4),))
    ancestor_blocks = draw_ancestor_blocks(jax.random.fold_in(key_list[8], 71), 0)
    visible_counts = draw_visible_counts(jax.random.fold_in(key_list[8], 71), 0)
    return dict(tokens=tokens, norm_gain=norm_gain, w_query=w_query, key_weight=key_weight, value_weight=value_weight, w_out=w_out, ancestor_blocks=ancestor_blocks, visible_counts=visible_counts)


ROPE_BASE = 500000.0
NORM_EPS = 1e-05

def rotary_apply(vectors, token_positions):
    midpoint = HEAD_SIZE // 2
    frequency = ROPE_BASE ** (-(jnp.arange(midpoint, dtype=jnp.float32) * 2.0) / HEAD_SIZE)
    angles = token_positions.astype(jnp.float32)[:, None] * frequency[None, :]
    cosine_part = jnp.cos(angles)[:, None, :]
    sine_part = jnp.sin(angles)[:, None, :]
    leading = vectors[..., :midpoint]
    trailing = vectors[..., midpoint:]
    return jnp.concatenate([leading * cosine_part - trailing * sine_part, trailing * cosine_part + leading * sine_part], axis=-1)

def attend_block(query_rows, own_keys, own_values, near_keys, near_values, seen):
    kv_cols = own_keys.shape[1]
    kv_heads = kv_cols // HEAD_SIZE
    group_size = query_rows.shape[1] // kv_cols
    key_count = (DEPTH + 1) * BLOCK_TOKENS
    all_keys = jnp.concatenate([near_keys.reshape(DEPTH * BLOCK_TOKENS, kv_cols), own_keys], axis=0).reshape(key_count, kv_heads, HEAD_SIZE)
    all_values = jnp.concatenate([near_values.reshape(DEPTH * BLOCK_TOKENS, kv_cols), own_values], axis=0).reshape(key_count, kv_heads, HEAD_SIZE)
    grouped = query_rows.reshape(BLOCK_TOKENS, kv_heads, group_size, HEAD_SIZE).transpose(1, 2, 0, 3).reshape(kv_heads, group_size * BLOCK_TOKENS, HEAD_SIZE)
    scores = jnp.einsum('gqd,kgd->gqk', grouped.astype(jnp.float32), all_keys.astype(jnp.float32), precision=lax.Precision.HIGHEST) * HEAD_SIZE ** (-0.5)
    key_index = jnp.arange(key_count, dtype=jnp.int32)
    key_slot = key_index // BLOCK_TOKENS
    key_offset = key_index % BLOCK_TOKENS
    limits = jnp.concatenate([seen.astype(jnp.int32), jnp.zeros((1,), jnp.int32)])[key_slot]
    query_offset = jnp.tile(jnp.arange(BLOCK_TOKENS, dtype=jnp.int32), group_size)
    allowed = jnp.where(key_slot[None, :] == DEPTH, key_offset[None, :] <= query_offset[:, None], (key_offset < limits)[None, :])
    masked = jnp.where(allowed[None], scores, -1e+30)
    row_max = lax.optimization_barrier(jnp.max(masked, axis=-1, keepdims=True))
    exponent = jnp.exp(masked - row_max)
    weights = (exponent / lax.optimization_barrier(jnp.sum(exponent, axis=-1, keepdims=True))).astype(jnp.bfloat16)
    mixed = jnp.einsum('gqk,kgd->gqd', weights.astype(jnp.float32), all_values.astype(jnp.float32), precision=lax.Precision.HIGHEST).astype(jnp.bfloat16)
    return mixed.reshape(kv_heads, group_size, BLOCK_TOKENS, HEAD_SIZE).transpose(2, 0, 1, 3).reshape(BLOCK_TOKENS, kv_heads * group_size * HEAD_SIZE)

def reference(tokens, norm_gain, w_query, key_weight, value_weight, w_out, ancestor_blocks, visible_counts):
    row_total = tokens.shape[0]
    block_total = row_total // BLOCK_TOKENS
    tok_float = tokens.astype(jnp.float32)
    mean_square = lax.optimization_barrier(jnp.mean(tok_float * tok_float, axis=1, keepdims=True))
    normed_input = (tok_float * lax.rsqrt(mean_square + NORM_EPS) * norm_gain).astype(jnp.bfloat16)
    base_pos = lax.optimization_barrier(jnp.sum(visible_counts, axis=1)).astype(jnp.int32)
    token_positions = (jnp.repeat(base_pos, BLOCK_TOKENS) + jnp.tile(jnp.arange(BLOCK_TOKENS, dtype=jnp.int32), block_total)).astype(jnp.int32)
    queries = jnp.dot(normed_input, w_query, preferred_element_type=jnp.float32).reshape(row_total, QUERY_HEADS, HEAD_SIZE)
    queries = rotary_apply(queries, token_positions).reshape(row_total, QUERY_HEADS * HEAD_SIZE).astype(jnp.bfloat16)
    key_rows = jnp.dot(normed_input, key_weight, preferred_element_type=jnp.float32).reshape(row_total, KEY_VALUE_HEADS, HEAD_SIZE)
    key_rows = rotary_apply(key_rows, token_positions).reshape(row_total, KEY_VALUE_HEADS * HEAD_SIZE).astype(jnp.bfloat16)
    value_rows = jnp.dot(normed_input, value_weight, preferred_element_type=jnp.float32).astype(jnp.bfloat16)
    blocked_keys = key_rows.reshape(block_total, BLOCK_TOKENS, KEY_VALUE_HEADS * HEAD_SIZE)
    blocked_values = value_rows.reshape(block_total, BLOCK_TOKENS, KEY_VALUE_HEADS * HEAD_SIZE)
    query_blocks = queries.reshape(block_total, BLOCK_TOKENS, QUERY_HEADS * HEAD_SIZE)

    def one_block(inputs):
        query_rows, own_keys, own_values, listed, seen = inputs
        picked = jnp.clip(listed, 0, block_total - 1).astype(jnp.int32)
        return attend_block(query_rows, own_keys, own_values, blocked_keys[picked], blocked_values[picked], seen)
    attention = lax.map(one_block, (query_blocks, blocked_keys, blocked_values, ancestor_blocks, visible_counts))
    attention = attention.reshape(row_total, QUERY_HEADS * HEAD_SIZE)
    group_cols = QUERY_HEADS * HEAD_SIZE // N_HEAD

    def add_group(running, group_id):
        columns = lax.dynamic_slice_in_dim(attention, group_id * group_cols, group_cols, 1)
        rows_part = lax.dynamic_slice_in_dim(w_out, group_id * group_cols, group_cols, 0)
        partial_term = jnp.dot(columns, rows_part, preferred_element_type=jnp.float32).astype(jnp.bfloat16)
        partial_term = lax.optimization_barrier(partial_term)
        return (running + partial_term.astype(jnp.float32), None)
    start_sum = jnp.zeros((row_total, MODEL_WIDTH), jnp.float32)
    summed, unused = lax.scan(add_group, start_sum, jnp.arange(N_HEAD, dtype=jnp.int32))
    return summed.astype(jnp.bfloat16)
```

```python
import functools

import numpy as np

import jax
import jax.numpy as jnp
from jax import lax
from jax.experimental import pallas as pl
from jax.experimental.pallas import tpu as pltpu
from jax.sharding import PartitionSpec as P

HEAD_SIZE = 128
BLOCK_TOKENS = 128
DEPTH = 8
ROPE_BASE = 500000.0
NORM_EPS = 1e-05
MESH = pl.DeviceIdType.MESH
SLOTS = DEPTH + 1
KEYS = SLOTS * BLOCK_TOKENS
LOG2E = 1.4426950408889634


def kernel(
    n_seq,
    n_head,
    tok_ref,
    gain_ref,
    freq_ref,
    wq_ref,
    wk_ref,
    wv_ref,
    wo_ref,
    anc_ref,
    vis_ref,
    out_ref,
    xbuf,
    wq,
    wk,
    wv,
    wo,
    normed,
    qbuf,
    kvbuf,
    kvcat,
    bias,
    attn,
    psend,
    precv,
    osum,
    acc,
    ysend,
    yrecv,
    w_sem,
    own_sem,
    ty_send,
    ty_recv,
    tc_send,
    tc_recv,
    tf_send,
    tf_recv,
    kz_send,
    kz_recv,
    kx_send,
    kx_recv,
    p_send,
    p_recv,
    r_send,
    r_recv,
):
    rows, width = tok_ref.shape
    blocks = rows // BLOCK_TOKENS
    q_cols = wq.shape[1]
    kv_cols = wk.shape[1]
    kv_heads = kv_cols // HEAD_SIZE
    group = q_cols // kv_cols
    ny = n_head // 2
    nx = ny
    nz = n_seq // nx
    seq = lax.axis_index("seq")
    head = lax.axis_index("head")
    y, core = lax.div(head, 2), lax.rem(head, 2)
    z, x = lax.div(seq, nx), lax.rem(seq, nx)
    partner = 2 * y + 1 - core

    def y_peer(j):
        return 2 * lax.rem(y + j, ny) + core

    def z_peer(j):
        return lax.rem(z + j, nz) * nx + x

    def x_peer(i):
        return z * nx + lax.rem(x + i, nx)

    def remote(src, dst, send, recv, seq_id, head_id):
        return pltpu.make_async_remote_copy(
            src_ref=src,
            dst_ref=dst,
            send_sem=send,
            recv_sem=recv,
            device_id=(seq_id, head_id),
            device_id_type=MESH,
        )

    barrier = pltpu.get_barrier_semaphore()
    peers = [(seq, partner)]
    peers += [(seq, y_peer(j)) for j in range(1, ny)]
    peers += [(z_peer(j), head) for j in range(1, nz)]
    peers += [(x_peer(i), head) for i in range(1, nx)]
    for peer in peers:
        pl.semaphore_signal(barrier, inc=1, device_id=peer, device_id_type=MESH)

    def weight_copy(i):
        source = (wk_ref, wv_ref, wq_ref, wo_ref)[i]
        return pltpu.make_async_copy(source, (wk, wv, wq, wo)[i], w_sem.at[i])

    def token_rows(b):
        return tok_ref.at[pl.ds(pl.multiple_of(b * BLOCK_TOKENS, BLOCK_TOKENS), BLOCK_TOKENS)]

    def own_copy(b):
        return pltpu.make_async_copy(token_rows(b), xbuf.at[b, head], own_sem.at[b])

    def tok_y(b, j):
        return remote(
            token_rows(b), xbuf.at[b, head], ty_send.at[b, j - 1], ty_recv.at[b, j - 1], seq, y_peer(j)
        )

    def tok_y_in(b, j):
        slot = xbuf.at[b, y_peer(ny - j)]
        return remote(slot, slot, ty_send.at[b, j - 1], ty_recv.at[b, j - 1], seq, y_peer(ny - j))

    def tok_core(b):
        return remote(token_rows(b), xbuf.at[b, head], tc_send.at[b], tc_recv.at[b], seq, partner)

    def tok_core_in(b):
        slot = xbuf.at[b, partner]
        return remote(slot, slot, tc_send.at[b], tc_recv.at[b], seq, partner)

    def tok_fwd(b, j):
        slot = xbuf.at[b, y_peer(ny - j)]
        return remote(slot, slot, tf_send.at[b, j - 1], tf_recv.at[b, j - 1], seq, partner)

    def tok_fwd_in(b, j):
        slot = xbuf.at[b, 2 * lax.rem(y + ny - j, ny) + 1 - core]
        return remote(slot, slot, tf_send.at[b, j - 1], tf_recv.at[b, j - 1], seq, partner)

    def kv_z(j):
        return remote(
            kvbuf.at[n_seq], kvbuf.at[seq], kz_send.at[j - 1], kz_recv.at[j - 1], z_peer(j), head
        )

    def kv_z_in(j):
        slot = kvbuf.at[z_peer(nz - j)]
        return remote(slot, slot, kz_send.at[j - 1], kz_recv.at[j - 1], z_peer(nz - j), head)

    def kv_x(j, i):
        src = kvbuf.at[n_seq] if j == 0 else kvbuf.at[z_peer(nz - j)]
        dst = kvbuf.at[seq] if j == 0 else kvbuf.at[z_peer(nz - j)]
        return remote(src, dst, kx_send.at[j, i - 1], kx_recv.at[j, i - 1], x_peer(i), head)

    def kv_x_in(j, i):
        slot = kvbuf.at[lax.rem(z + nz - j, nz) * nx + lax.rem(x + nx - i, nx)]
        return remote(slot, slot, kx_send.at[j, i - 1], kx_recv.at[j, i - 1], x_peer(nx - i), head)

    def part_core(b):
        return remote(psend.at[b], precv.at[b], p_send.at[b], p_recv.at[b], seq, partner)

    def part_y(b, j):
        return remote(
            ysend.at[b, j - 1],
            yrecv.at[b, j - 1],
            r_send.at[b, j - 1],
            r_recv.at[b, j - 1],
            seq,
            y_peer(j),
        )

    for b in range(blocks):
        own_copy(b).start()
    for i in range(4):
        weight_copy(i).start()
    pl.semaphore_wait(barrier, len(peers))
    for b in range(blocks):
        for j in range(1, ny):
            tok_y(b, j).start()
        tok_core(b).start()

    def project(b, carry):
        for j in range(1, ny):
            tok_y_in(b, j).wait_recv()
            tok_fwd(b, j).start()
        own_copy(b).wait()
        tok_core_in(b).wait_recv()

        @pl.when(b == 2)
        def _():
            for j in range(1, nz):
                kv_z_in(j).wait_recv()
                for i in range(1, nx):
                    kv_x(j, i).start()

        for j in range(1, ny):
            tok_fwd_in(b, j).wait_recv()

        square = jnp.zeros((BLOCK_TOKENS, 1), jnp.float32)
        for k in range(n_head):
            piece = xbuf[b, k].astype(jnp.float32)
            square += jnp.sum(piece * piece, axis=1, keepdims=True)
        scale = lax.rsqrt(square / (n_head * width) + NORM_EPS)
        for k in range(n_head):
            piece = xbuf[b, k].astype(jnp.float32)
            cols = slice(k * width, (k + 1) * width)
            normed[:, cols] = (piece * scale * gain_ref[:, cols]).astype(jnp.bfloat16)

        base = vis_ref[b, 0]
        for j in range(1, DEPTH):
            base += vis_ref[b, j]
        position = base + lax.broadcasted_iota(jnp.int32, (BLOCK_TOKENS, HEAD_SIZE), 0)
        angle = position.astype(jnp.float32) * freq_ref[...]
        lane = lax.broadcasted_iota(jnp.int32, (BLOCK_TOKENS, HEAD_SIZE), 1)
        cosine = jnp.cos(angle)
        sine = jnp.sin(angle)
        sine = jnp.where(lane < HEAD_SIZE // 2, -sine, sine)

        def rope(vectors):
            return vectors * cosine + pltpu.roll(vectors, HEAD_SIZE // 2, 1) * sine

        @pl.when(b == 0)
        def _():
            weight_copy(0).wait()
            weight_copy(1).wait()

        keys = jnp.dot(normed[...], wk[...], preferred_element_type=jnp.float32)
        for g in range(kv_heads):
            cols = slice(g * HEAD_SIZE, (g + 1) * HEAD_SIZE)
            kvbuf[n_seq + b, :, cols] = rope(keys[:, cols]).astype(jnp.bfloat16)
        values = jnp.dot(normed[...], wv[...], preferred_element_type=jnp.float32)
        kvbuf[n_seq + b, :, kv_cols:] = values.astype(jnp.bfloat16)

        @pl.when(b == 0)
        def _():
            for j in range(1, nz):
                kv_z(j).start()
            for i in range(1, nx):
                kv_x(0, i).start()
            weight_copy(2).wait()

        tile = 2 * HEAD_SIZE

        def query_tile(t, inner):
            cols = pl.ds(pl.multiple_of(t * tile, tile), tile)
            found = jnp.dot(normed[...], wq[:, cols], preferred_element_type=jnp.float32)
            for k in range(2):
                turned = rope(found[:, k * HEAD_SIZE : (k + 1) * HEAD_SIZE])
                qbuf[b, 2 * t + k] = (turned * (HEAD_SIZE**-0.5 * LOG2E)).astype(jnp.bfloat16)
            return inner

        lax.fori_loop(0, q_cols // tile, query_tile, 0)
        return carry

    lax.fori_loop(0, blocks, project, 0)

    weight_copy(3).wait()
    for j in range(nz):
        for i in range(1, nx):
            kv_x_in(j, i).wait_recv()

    def attend(b, carry):
        lane = lax.broadcasted_iota(jnp.int32, (BLOCK_TOKENS, BLOCK_TOKENS), 1)
        row = lax.broadcasted_iota(jnp.int32, (BLOCK_TOKENS, BLOCK_TOKENS), 0)
        for j in range(SLOTS):
            part = slice(j * BLOCK_TOKENS, (j + 1) * BLOCK_TOKENS)
            if j < DEPTH:
                block_id = jnp.maximum(anc_ref[b, j], 0)
                owner, inside = lax.div(block_id, blocks), lax.rem(block_id, blocks)
                slot = jnp.where(owner == seq, n_seq + inside, owner)
                allowed = lane < vis_ref[b, j]
            else:
                slot = n_seq + b
                allowed = lane <= row
            kvcat[part] = kvbuf[slot]
            bias[:, part] = jnp.where(allowed, 0.0, -1e30)

        for g in range(kv_heads):
            query = qbuf[b, g * group : (g + 1) * group].reshape(
                group * BLOCK_TOKENS, HEAD_SIZE
            )
            key = kvcat[:, g * HEAD_SIZE : (g + 1) * HEAD_SIZE]
            value = kvcat[:, kv_cols + g * HEAD_SIZE : kv_cols + (g + 1) * HEAD_SIZE]
            scores = lax.dot_general(
                query, key, (((1,), (1,)), ((), ())), preferred_element_type=jnp.float32
            )
            scores = (
                scores.reshape(group, BLOCK_TOKENS, KEYS) + bias[...][None]
            ).reshape(group * BLOCK_TOKENS, KEYS)
            top = jnp.max(scores, axis=1, keepdims=True)
            weight = jnp.exp2(scores - top)
            total = jnp.sum(weight, axis=1, keepdims=True)
            mixed = jnp.dot(
                weight.astype(jnp.bfloat16), value, preferred_element_type=jnp.float32
            )
            mixed = (mixed / total).astype(jnp.bfloat16)
            for k in range(group):
                at = (g * group + k) * HEAD_SIZE
                attn[:, at : at + HEAD_SIZE] = mixed[k * BLOCK_TOKENS : (k + 1) * BLOCK_TOKENS]

        tile = 512
        per = width // tile

        def other_tile(t, inner):
            k, m = lax.div(t, per), lax.rem(t, per)
            cols = pl.ds(pl.multiple_of((2 * k + 1 - core) * width + m * tile, tile), tile)
            into = pl.ds(pl.multiple_of(m * tile, tile), tile)
            found = jnp.dot(attn[...], wo[:, cols], preferred_element_type=jnp.float32)
            psend[b, k, :, into] = found.astype(jnp.bfloat16)
            return inner

        lax.fori_loop(0, ny * per, other_tile, 0)
        part_core(b).start()

        def own_tile(t, inner):
            k, m = lax.div(t, per), lax.rem(t, per)
            cols = pl.ds(pl.multiple_of((2 * k + core) * width + m * tile, tile), tile)
            into = pl.ds(pl.multiple_of(m * tile, tile), tile)
            osum[k, :, into] = jnp.dot(attn[...], wo[:, cols], preferred_element_type=jnp.float32)
            return inner

        lax.fori_loop(0, ny * per, own_tile, 0)
        part_core(b).wait_recv()
        for j in range(1, ny):
            k = lax.rem(y + j, ny)
            ysend[b, j - 1] = (osum[k] + precv[b, k].astype(jnp.float32)).astype(jnp.bfloat16)
            part_y(b, j).start()
        acc[b] = osum[y] + precv[b, y].astype(jnp.float32)
        return carry

    lax.fori_loop(0, blocks, attend, 0)

    def finish(b, carry):
        result = acc[b]
        for j in range(1, ny):
            part_y(b, j).wait_recv()
            result += yrecv[b, j - 1].astype(jnp.float32)
        out_ref[pl.ds(pl.multiple_of(b * BLOCK_TOKENS, BLOCK_TOKENS), BLOCK_TOKENS)] = (
            result.astype(jnp.bfloat16)
        )
        for j in range(1, ny):
            tok_y(b, j).wait_send()
            tok_fwd(b, j).wait_send()
            part_y(b, j).wait_send()
        tok_core(b).wait_send()
        part_core(b).wait_send()
        return carry

    lax.fori_loop(0, blocks, finish, 0)
    for j in range(1, nz):
        kv_z(j).wait_send()
    for j in range(nz):
        for i in range(1, nx):
            kv_x(j, i).wait_send()


def local(
    n_seq,
    n_head,
    tokens,
    norm_gain,
    w_query,
    key_weight,
    value_weight,
    w_out,
    ancestor_blocks,
    visible_counts,
):
    rows, width = tokens.shape
    blocks = rows // BLOCK_TOKENS
    q_cols = w_query.shape[1]
    kv_cols = key_weight.shape[1]
    ny = n_head // 2
    nx = ny
    nz = n_seq // nx
    half = HEAD_SIZE // 2
    frequency = ROPE_BASE ** (-(np.arange(half) * 2.0) / HEAD_SIZE)
    frequency = np.concatenate([frequency, frequency]).astype(np.float32)[None]
    dma = pltpu.SemaphoreType.DMA
    vmem = pl.BlockSpec(memory_space=pltpu.VMEM)
    smem = pl.BlockSpec(memory_space=pltpu.SMEM)
    hbm = pl.BlockSpec(memory_space=pl.ANY)
    bf16, f32 = jnp.bfloat16, jnp.float32
    return pl.pallas_call(
        functools.partial(kernel, n_seq, n_head),
        out_shape=jax.ShapeDtypeStruct((rows, width), bf16),
        in_specs=[hbm, vmem, vmem, hbm, hbm, hbm, hbm, smem, smem],
        out_specs=vmem,
        scratch_shapes=[
            pltpu.VMEM((blocks, n_head, BLOCK_TOKENS, width), bf16),
            pltpu.VMEM(w_query.shape, bf16),
            pltpu.VMEM(key_weight.shape, bf16),
            pltpu.VMEM(value_weight.shape, bf16),
            pltpu.VMEM(w_out.shape, bf16),
            pltpu.VMEM((BLOCK_TOKENS, n_head * width), bf16),
            pltpu.VMEM((blocks, q_cols // HEAD_SIZE, BLOCK_TOKENS, HEAD_SIZE), bf16),
            pltpu.VMEM((n_seq + blocks, BLOCK_TOKENS, 2 * kv_cols), bf16),
            pltpu.VMEM((KEYS, 2 * kv_cols), bf16),
            pltpu.VMEM((BLOCK_TOKENS, KEYS), f32),
            pltpu.VMEM((BLOCK_TOKENS, q_cols), bf16),
            pltpu.VMEM((blocks, ny, BLOCK_TOKENS, width), bf16),
            pltpu.VMEM((blocks, ny, BLOCK_TOKENS, width), bf16),
            pltpu.VMEM((ny, BLOCK_TOKENS, width), f32),
            pltpu.VMEM((blocks, BLOCK_TOKENS, width), f32),
            pltpu.VMEM((blocks, ny - 1, BLOCK_TOKENS, width), bf16),
            pltpu.VMEM((blocks, ny - 1, BLOCK_TOKENS, width), bf16),
            dma((4,)),
            dma((blocks,)),
            dma((blocks, ny - 1)),
            dma((blocks, ny - 1)),
            dma((blocks,)),
            dma((blocks,)),
            dma((blocks, ny - 1)),
            dma((blocks, ny - 1)),
            dma((nz - 1,)),
            dma((nz - 1,)),
            dma((nz, nx - 1)),
            dma((nz, nx - 1)),
            dma((blocks,)),
            dma((blocks,)),
            dma((blocks, ny - 1)),
            dma((blocks, ny - 1)),
        ],
        compiler_params=pltpu.CompilerParams(
            collective_id=0, has_side_effects=True, vmem_limit_bytes=60 * 1024 * 1024
        ),
        cost_estimate=pl.CostEstimate(
            flops=13 * 10**9, bytes_accessed=25 * 10**6, transcendentals=5 * 10**6
        ),
    )(
        tokens,
        norm_gain[None],
        jnp.asarray(frequency),
        w_query,
        key_weight,
        value_weight,
        w_out,
        ancestor_blocks,
        visible_counts,
    )


def solution(mesh):
    placed = (
        P("seq", "head"),
        P(),
        P(None, "head"),
        P(None, "head"),
        P(None, "head"),
        P("head", None),
        P("seq", None),
        P("seq", None),
    )
    return jax.shard_map(
        functools.partial(local, mesh.shape["seq"], mesh.shape["head"]),
        mesh=mesh,
        in_specs=placed,
        out_specs=P("seq", "head"),
        check_vma=False,
    )
```

```python
import functools

import numpy as np

import jax
import jax.numpy as jnp
from jax import lax
from jax.experimental import pallas as pl
from jax.experimental.pallas import tpu as pltpu
from jax.sharding import PartitionSpec as P

HEAD_SIZE = 128
BLOCK_TOKENS = 128
DEPTH = 8
ROPE_BASE = 500000.0
NORM_EPS = 1e-05
MESH = pl.DeviceIdType.MESH
SLOTS = DEPTH + 1
KEYS = SLOTS * BLOCK_TOKENS
LOG2E = 1.4426950408889634
MASKED = -1e30


def kernel(
    n_seq,
    n_head,
    tok_ref,
    gain_ref,
    freq_ref,
    wq_ref,
    wk_ref,
    wv_ref,
    wo_ref,
    anc_ref,
    vis_ref,
    out_ref,
    xbuf,
    wq,
    wk,
    wv,
    wo,
    normed,
    qbuf,
    kvbuf,
    kcat,
    vcat,
    attn,
    psend,
    precv,
    acc,
    ysend,
    yrecv,
    w_sem,
    own_sem,
    ty_send,
    ty_recv,
    tc_send,
    tc_recv,
    tf_send,
    tf_recv,
    kz_send,
    kz_recv,
    kx_send,
    kx_recv,
    p_send,
    p_recv,
    r_send,
    r_recv,
):
    rows, width = tok_ref.shape
    blocks = rows // BLOCK_TOKENS
    q_cols = wq.shape[1]
    kv_cols = wk.shape[1]
    kv_heads = kv_cols // HEAD_SIZE
    group = q_cols // kv_cols
    ny = n_head // 2
    nx = ny
    nz = n_seq // nx
    seq = lax.axis_index("seq")
    head = lax.axis_index("head")
    y, core = lax.div(head, 2), lax.rem(head, 2)
    z, x = lax.div(seq, nx), lax.rem(seq, nx)
    partner = 2 * y + 1 - core

    def y_peer(j):
        return 2 * lax.rem(y + j, ny) + core

    def z_peer(j):
        return lax.rem(z + j, nz) * nx + x

    def x_peer(i):
        return z * nx + lax.rem(x + i, nx)

    def remote(src, dst, send, recv, seq_id, head_id):
        return pltpu.make_async_remote_copy(
            src_ref=src,
            dst_ref=dst,
            send_sem=send,
            recv_sem=recv,
            device_id=(seq_id, head_id),
            device_id_type=MESH,
        )

    barrier = pltpu.get_barrier_semaphore()
    peers = [(seq, partner)]
    peers += [(seq, y_peer(j)) for j in range(1, ny)]
    peers += [(z_peer(j), head) for j in range(1, nz)]
    peers += [(x_peer(i), head) for i in range(1, nx)]
    for peer in peers:
        pl.semaphore_signal(barrier, inc=1, device_id=peer, device_id_type=MESH)

    def weight_copy(i):
        source = (wk_ref, wv_ref, wq_ref, wo_ref)[i]
        return pltpu.make_async_copy(source, (wk, wv, wq, wo)[i], w_sem.at[i])

    def token_rows(b):
        return tok_ref.at[pl.ds(pl.multiple_of(b * BLOCK_TOKENS, BLOCK_TOKENS), BLOCK_TOKENS)]

    def own_copy(b):
        return pltpu.make_async_copy(token_rows(b), xbuf.at[b, head], own_sem.at[b])

    def tok_y(b, j):
        return remote(
            token_rows(b), xbuf.at[b, head], ty_send.at[b, j - 1], ty_recv.at[b, j - 1], seq, y_peer(j)
        )

    def tok_y_in(b, j):
        slot = xbuf.at[b, y_peer(ny - j)]
        return remote(slot, slot, ty_send.at[b, j - 1], ty_recv.at[b, j - 1], seq, y_peer(ny - j))

    def tok_core(b):
        return remote(token_rows(b), xbuf.at[b, head], tc_send.at[b], tc_recv.at[b], seq, partner)

    def tok_core_in(b):
        slot = xbuf.at[b, partner]
        return remote(slot, slot, tc_send.at[b], tc_recv.at[b], seq, partner)

    def tok_fwd(b, j):
        slot = xbuf.at[b, y_peer(ny - j)]
        return remote(slot, slot, tf_send.at[b, j - 1], tf_recv.at[b, j - 1], seq, partner)

    def tok_fwd_in(b, j):
        slot = xbuf.at[b, 2 * lax.rem(y + ny - j, ny) + 1 - core]
        return remote(slot, slot, tf_send.at[b, j - 1], tf_recv.at[b, j - 1], seq, partner)

    def kv_z(j):
        return remote(
            kvbuf.at[n_seq], kvbuf.at[seq], kz_send.at[j - 1], kz_recv.at[j - 1], z_peer(j), head
        )

    def kv_z_in(j):
        slot = kvbuf.at[z_peer(nz - j)]
        return remote(slot, slot, kz_send.at[j - 1], kz_recv.at[j - 1], z_peer(nz - j), head)

    def kv_x(j, i):
        src = kvbuf.at[n_seq] if j == 0 else kvbuf.at[z_peer(nz - j)]
        dst = kvbuf.at[seq] if j == 0 else kvbuf.at[z_peer(nz - j)]
        return remote(src, dst, kx_send.at[j, i - 1], kx_recv.at[j, i - 1], x_peer(i), head)

    def kv_x_in(j, i):
        slot = kvbuf.at[lax.rem(z + nz - j, nz) * nx + lax.rem(x + nx - i, nx)]
        return remote(slot, slot, kx_send.at[j, i - 1], kx_recv.at[j, i - 1], x_peer(nx - i), head)

    def part_core(b, j):
        return remote(
            psend.at[b, j], precv.at[b, j], p_send.at[b, j], p_recv.at[b, j], seq, partner
        )

    def part_y(b, j):
        return remote(
            ysend.at[b, j - 1],
            yrecv.at[b, j - 1],
            r_send.at[b, j - 1],
            r_recv.at[b, j - 1],
            seq,
            y_peer(j),
        )

    def send_tokens(b):
        for j in range(1, ny):
            tok_y(b, j).start()
        tok_core(b).start()

    own_copy(0).start()
    weight_copy(0).start()
    weight_copy(1).start()

    lane = lax.broadcasted_iota(jnp.int32, (BLOCK_TOKENS, BLOCK_TOKENS), 1)
    row = lax.broadcasted_iota(jnp.int32, (BLOCK_TOKENS, BLOCK_TOKENS), 0)
    identity = jnp.where(lane == row, 1.0, 0.0).astype(jnp.bfloat16)
    causal = jnp.where(row <= lane, 0.0, MASKED).astype(jnp.bfloat16)

    def fill(b, carry):
        for k in range(q_cols // HEAD_SIZE):
            qbuf[b, k, :, HEAD_SIZE:] = identity
        return carry

    lax.fori_loop(0, blocks, fill, 0)
    for g in range(kv_heads):
        kcat[g, DEPTH * BLOCK_TOKENS :, HEAD_SIZE:] = causal
        vcat[g, :, HEAD_SIZE:] = jnp.ones((KEYS, HEAD_SIZE), jnp.bfloat16)

    pl.semaphore_wait(barrier, len(peers))
    send_tokens(0)
    weight_copy(2).start()
    for b in range(1, blocks):
        own_copy(b).start()

    def project(b, carry):
        for j in range(1, ny):
            tok_y_in(b, j).wait_recv()
            tok_fwd(b, j).start()

        @pl.when(b < blocks - 1)
        def _():
            send_tokens(b + 1)

        @pl.when(b == 1)
        def _():
            weight_copy(3).start()

        own_copy(b).wait()
        tok_core_in(b).wait_recv()

        @pl.when(b == 2)
        def _():
            for j in range(1, nz):
                kv_z_in(j).wait_recv()
                for i in range(1, nx):
                    kv_x(j, i).start()

        for j in range(1, ny):
            tok_fwd_in(b, j).wait_recv()

        square = jnp.zeros((BLOCK_TOKENS, 1), jnp.float32)
        for k in range(n_head):
            piece = xbuf[b, k].astype(jnp.float32)
            square += jnp.sum(piece * piece, axis=1, keepdims=True)
        scale = lax.rsqrt(square / (n_head * width) + NORM_EPS)
        for k in range(n_head):
            piece = xbuf[b, k].astype(jnp.float32)
            cols = slice(k * width, (k + 1) * width)
            normed[:, cols] = (piece * scale * gain_ref[:, cols]).astype(jnp.bfloat16)

        base = vis_ref[b, 0]
        for j in range(1, DEPTH):
            base += vis_ref[b, j]
        position = base + lax.broadcasted_iota(jnp.int32, (BLOCK_TOKENS, HEAD_SIZE), 0)
        angle = position.astype(jnp.float32) * freq_ref[...]
        cosine = jnp.cos(angle)
        sine = jnp.sin(angle)
        sine = jnp.where(lane < HEAD_SIZE // 2, -sine, sine)

        def rope(vectors):
            return vectors * cosine + pltpu.roll(vectors, HEAD_SIZE // 2, 1) * sine

        @pl.when(b == 0)
        def _():
            weight_copy(0).wait()
            weight_copy(1).wait()

        keys = jnp.dot(normed[...], wk[...], preferred_element_type=jnp.float32)
        for g in range(kv_heads):
            cols = slice(g * HEAD_SIZE, (g + 1) * HEAD_SIZE)
            kvbuf[n_seq + b, :, cols] = rope(keys[:, cols]).astype(jnp.bfloat16)
        values = jnp.dot(normed[...], wv[...], preferred_element_type=jnp.float32)
        kvbuf[n_seq + b, :, kv_cols:] = values.astype(jnp.bfloat16)

        @pl.when(b == 0)
        def _():
            for j in range(1, nz):
                kv_z(j).start()
            for i in range(1, nx):
                kv_x(0, i).start()
            weight_copy(2).wait()

        tile = 2 * HEAD_SIZE

        def query_tile(t, inner):
            cols = pl.ds(pl.multiple_of(t * tile, tile), tile)
            found = jnp.dot(normed[...], wq[:, cols], preferred_element_type=jnp.float32)
            for k in range(2):
                turned = rope(found[:, k * HEAD_SIZE : (k + 1) * HEAD_SIZE])
                qbuf[b, 2 * t + k, :, :HEAD_SIZE] = (turned * (HEAD_SIZE**-0.5 * LOG2E)).astype(
                    jnp.bfloat16
                )
            return inner

        lax.fori_loop(0, q_cols // tile, query_tile, 0)
        return carry

    lax.fori_loop(0, blocks, project, 0)

    weight_copy(3).wait()
    for j in range(nz):
        for i in range(1, nx):
            kv_x_in(j, i).wait_recv()

    def attend(b, carry):
        for j in range(SLOTS):
            part = slice(j * BLOCK_TOKENS, (j + 1) * BLOCK_TOKENS)
            if j < DEPTH:
                block_id = jnp.maximum(anc_ref[b, j], 0)
                owner, inside = lax.div(block_id, blocks), lax.rem(block_id, blocks)
                slot = jnp.where(owner == seq, n_seq + inside, owner)
                mask = jnp.where(row < vis_ref[b, j], 0.0, MASKED).astype(jnp.bfloat16)
            else:
                slot = n_seq + b
            for g in range(kv_heads):
                cols = slice(g * HEAD_SIZE, (g + 1) * HEAD_SIZE)
                kcat[g, part, :HEAD_SIZE] = kvbuf[slot, :, cols]
                cols = slice(kv_cols + g * HEAD_SIZE, kv_cols + (g + 1) * HEAD_SIZE)
                vcat[g, part, :HEAD_SIZE] = kvbuf[slot, :, cols]
                if j < DEPTH:
                    kcat[g, part, HEAD_SIZE:] = mask

        for g in range(kv_heads):
            query = qbuf[b, g * group : (g + 1) * group].reshape(
                group * BLOCK_TOKENS, 2 * HEAD_SIZE
            )
            scores = lax.dot_general(
                query, kcat[g], (((1,), (1,)), ((), ())), preferred_element_type=jnp.float32
            )
            top = jnp.max(scores, axis=1, keepdims=True)
            weight = jnp.exp2(scores - top).astype(jnp.bfloat16)
            mixed = jnp.dot(weight, vcat[g], preferred_element_type=jnp.float32)
            mixed = (mixed[:, :HEAD_SIZE] / mixed[:, HEAD_SIZE:]).astype(jnp.bfloat16)
            for k in range(group):
                at = (g * group + k) * HEAD_SIZE
                attn[:, at : at + HEAD_SIZE] = mixed[k * BLOCK_TOKENS : (k + 1) * BLOCK_TOKENS]

        tile = 512

        def share(j, side, store):
            base = (2 * lax.rem(y + j, ny) + side) * width

            def one_tile(t, inner):
                cols = pl.ds(pl.multiple_of(base + t * tile, tile), tile)
                into = pl.ds(pl.multiple_of(t * tile, tile), tile)
                store(into, jnp.dot(attn[...], wo[:, cols], preferred_element_type=jnp.float32))
                return inner

            lax.fori_loop(0, width // tile, one_tile, 0)

        def other_share(j):
            def store(into, found):
                psend[b, j, :, into] = found.astype(jnp.bfloat16)

            share(j, 1 - core, store)
            part_core(b, j).start()

        for j in range(1, ny):
            other_share(j)
        for j in range(1, ny):

            def add(into, found):
                acc[b, :, into] = found

            share(j, core, add)
            part_core(b, j).wait_recv()
            ysend[b, j - 1] = (acc[b] + precv[b, j].astype(jnp.float32)).astype(jnp.bfloat16)
            part_y(b, j).start()
        other_share(0)

        def keep(into, found):
            acc[b, :, into] = found

        share(0, core, keep)
        return carry

    lax.fori_loop(0, blocks, attend, 0)

    def finish(b, carry):
        part_core(b, 0).wait_recv()
        result = acc[b] + precv[b, 0].astype(jnp.float32)
        for j in range(1, ny):
            part_y(b, j).wait_recv()
            result += yrecv[b, j - 1].astype(jnp.float32)
        out_ref[pl.ds(pl.multiple_of(b * BLOCK_TOKENS, BLOCK_TOKENS), BLOCK_TOKENS)] = (
            result.astype(jnp.bfloat16)
        )
        for j in range(1, ny):
            tok_y(b, j).wait_send()
            tok_fwd(b, j).wait_send()
            part_y(b, j).wait_send()
        tok_core(b).wait_send()
        for j in range(ny):
            part_core(b, j).wait_send()
        return carry

    lax.fori_loop(0, blocks, finish, 0)
    for j in range(1, nz):
        kv_z(j).wait_send()
    for j in range(nz):
        for i in range(1, nx):
            kv_x(j, i).wait_send()


def local(
    n_seq,
    n_head,
    tokens,
    norm_gain,
    w_query,
    key_weight,
    value_weight,
    w_out,
    ancestor_blocks,
    visible_counts,
):
    rows, width = tokens.shape
    blocks = rows // BLOCK_TOKENS
    q_cols = w_query.shape[1]
    kv_cols = key_weight.shape[1]
    ny = n_head // 2
    nx = ny
    nz = n_seq // nx
    half = HEAD_SIZE // 2
    frequency = ROPE_BASE ** (-(np.arange(half) * 2.0) / HEAD_SIZE)
    frequency = np.concatenate([frequency, frequency]).astype(np.float32)[None]
    dma = pltpu.SemaphoreType.DMA
    vmem = pl.BlockSpec(memory_space=pltpu.VMEM)
    smem = pl.BlockSpec(memory_space=pltpu.SMEM)
    hbm = pl.BlockSpec(memory_space=pl.ANY)
    bf16, f32 = jnp.bfloat16, jnp.float32
    return pl.pallas_call(
        functools.partial(kernel, n_seq, n_head),
        out_shape=jax.ShapeDtypeStruct((rows, width), bf16),
        in_specs=[hbm, vmem, vmem, hbm, hbm, hbm, hbm, smem, smem],
        out_specs=vmem,
        scratch_shapes=[
            pltpu.VMEM((blocks, n_head, BLOCK_TOKENS, width), bf16),
            pltpu.VMEM(w_query.shape, bf16),
            pltpu.VMEM(key_weight.shape, bf16),
            pltpu.VMEM(value_weight.shape, bf16),
            pltpu.VMEM(w_out.shape, bf16),
            pltpu.VMEM((BLOCK_TOKENS, n_head * width), bf16),
            pltpu.VMEM((blocks, q_cols // HEAD_SIZE, BLOCK_TOKENS, 2 * HEAD_SIZE), bf16),
            pltpu.VMEM((n_seq + blocks, BLOCK_TOKENS, 2 * kv_cols), bf16),
            pltpu.VMEM((kv_cols // HEAD_SIZE, KEYS, 2 * HEAD_SIZE), bf16),
            pltpu.VMEM((kv_cols // HEAD_SIZE, KEYS, 2 * HEAD_SIZE), bf16),
            pltpu.VMEM((BLOCK_TOKENS, q_cols), bf16),
            pltpu.VMEM((blocks, ny, BLOCK_TOKENS, width), bf16),
            pltpu.VMEM((blocks, ny, BLOCK_TOKENS, width), bf16),
            pltpu.VMEM((blocks, BLOCK_TOKENS, width), f32),
            pltpu.VMEM((blocks, ny - 1, BLOCK_TOKENS, width), bf16),
            pltpu.VMEM((blocks, ny - 1, BLOCK_TOKENS, width), bf16),
            dma((4,)),
            dma((blocks,)),
            dma((blocks, ny - 1)),
            dma((blocks, ny - 1)),
            dma((blocks,)),
            dma((blocks,)),
            dma((blocks, ny - 1)),
            dma((blocks, ny - 1)),
            dma((nz - 1,)),
            dma((nz - 1,)),
            dma((nz, nx - 1)),
            dma((nz, nx - 1)),
            dma((blocks, ny)),
            dma((blocks, ny)),
            dma((blocks, ny - 1)),
            dma((blocks, ny - 1)),
        ],
        compiler_params=pltpu.CompilerParams(
            collective_id=0, has_side_effects=True, vmem_limit_bytes=60 * 1024 * 1024
        ),
        cost_estimate=pl.CostEstimate(
            flops=13 * 10**9, bytes_accessed=25 * 10**6, transcendentals=5 * 10**6
        ),
    )(
        tokens,
        norm_gain[None],
        jnp.asarray(frequency),
        w_query,
        key_weight,
        value_weight,
        w_out,
        ancestor_blocks,
        visible_counts,
    )


def solution(mesh):
    placed = (
        P("seq", "head"),
        P(),
        P(None, "head"),
        P(None, "head"),
        P(None, "head"),
        P("head", None),
        P("seq", None),
        P("seq", None),
    )
    return jax.shard_map(
        functools.partial(local, mesh.shape["seq"], mesh.shape["head"]),
        mesh=mesh,
        in_specs=placed,
        out_specs=P("seq", "head"),
        check_vma=False,
    )
```

```python
import functools

import numpy as np

import jax
import jax.numpy as jnp
from jax import lax
from jax.experimental import pallas as pl
from jax.experimental.pallas import tpu as pltpu
from jax.sharding import PartitionSpec as P

HEAD_SIZE = 128
BLOCK_TOKENS = 128
DEPTH = 8
ROPE_BASE = 500000.0
NORM_EPS = 1e-05
MESH = pl.DeviceIdType.MESH
SLOTS = DEPTH + 1
KEYS = SLOTS * BLOCK_TOKENS
LOG2E = 1.4426950408889634
MASKED = -1e30


def kernel(
    n_seq,
    n_head,
    tok_ref,
    gain_ref,
    freq_ref,
    wq_ref,
    wk_ref,
    wv_ref,
    wo_ref,
    anc_ref,
    vis_ref,
    out_ref,
    xbuf,
    wq,
    wk,
    wv,
    wo,
    scaled,
    part,
    square,
    cosine,
    sine,
    qbuf,
    kvbuf,
    kcat,
    vcat,
    attn,
    psend,
    precv,
    acc,
    ysend,
    yrecv,
    w_sem,
    o_sem,
    own_sem,
    ty_send,
    ty_recv,
    tc_send,
    tc_recv,
    tf_send,
    tf_recv,
    kz_send,
    kz_recv,
    kx_send,
    kx_recv,
    p_send,
    p_recv,
    r_send,
    r_recv,
):
    rows, width = tok_ref.shape
    blocks = rows // BLOCK_TOKENS
    q_cols = wq.shape[2]
    kv_cols = wk.shape[2]
    kv_heads = kv_cols // HEAD_SIZE
    group = q_cols // kv_cols
    ny = n_head // 2
    nx = ny
    nz = n_seq // nx
    seq = lax.axis_index("seq")
    head = lax.axis_index("head")
    y, core = lax.div(head, 2), lax.rem(head, 2)
    z, x = lax.div(seq, nx), lax.rem(seq, nx)
    partner = 2 * y + 1 - core

    def y_peer(j):
        return 2 * lax.rem(y + j, ny) + core

    def z_peer(j):
        return lax.rem(z + j, nz) * nx + x

    def x_peer(i):
        return z * nx + lax.rem(x + i, nx)

    def remote(src, dst, send, recv, seq_id, head_id):
        return pltpu.make_async_remote_copy(
            src_ref=src,
            dst_ref=dst,
            send_sem=send,
            recv_sem=recv,
            device_id=(seq_id, head_id),
            device_id_type=MESH,
        )

    barrier = pltpu.get_barrier_semaphore()
    peers = [(seq, partner)]
    peers += [(seq, y_peer(j)) for j in range(1, ny)]
    peers += [(z_peer(j), head) for j in range(1, nz)]
    peers += [(x_peer(i), head) for i in range(1, nx)]
    for peer in peers:
        pl.semaphore_signal(barrier, inc=1, device_id=peer, device_id_type=MESH)

    def weight_copy(i, j):
        source = (wk_ref, wv_ref, wq_ref)[i]
        first = pl.multiple_of(2 * width * lax.rem(y + j, ny), 2 * width)
        return pltpu.make_async_copy(
            source.at[pl.ds(first, 2 * width)], (wk, wv, wq)[i].at[j], w_sem.at[i, j]
        )

    def out_copy():
        return pltpu.make_async_copy(wo_ref, wo, o_sem)

    def block_rows(b):
        return pl.ds(pl.multiple_of(b * BLOCK_TOKENS, BLOCK_TOKENS), BLOCK_TOKENS)

    def own_copy():
        return pltpu.make_async_copy(tok_ref, xbuf.at[0, core], own_sem)

    def tok_y(b, j):
        return remote(
            tok_ref.at[block_rows(b)],
            xbuf.at[ny - j, core, block_rows(b)],
            ty_send.at[b, j - 1],
            ty_recv.at[b, j - 1],
            seq,
            y_peer(j),
        )

    def tok_core():
        return remote(tok_ref, xbuf.at[0, core], tc_send, tc_recv, seq, partner)

    def tok_core_in():
        slot = xbuf.at[0, 1 - core]
        return remote(slot, slot, tc_send, tc_recv, seq, partner)

    def tok_fwd(b, j):
        slot = xbuf.at[ny - j, core, block_rows(b)]
        return remote(slot, slot, tf_send.at[b, j - 1], tf_recv.at[b, j - 1], seq, partner)

    def tok_fwd_in(b, j):
        slot = xbuf.at[ny - j, 1 - core, block_rows(b)]
        return remote(slot, slot, tf_send.at[b, j - 1], tf_recv.at[b, j - 1], seq, partner)

    def kv_z(to):
        return remote(
            kvbuf.at[n_seq], kvbuf.at[seq], kz_send.at[to], kz_recv.at[z], to * nx + x, head
        )

    def kv_z_in(source):
        slot = kvbuf.at[source * nx + x]
        return remote(slot, slot, kz_send.at[source], kz_recv.at[source], source * nx + x, head)

    def kv_x(source, i, own):
        slot = kvbuf.at[source * nx + x]
        src = kvbuf.at[n_seq] if own else slot
        return remote(
            src, slot, kx_send.at[source, i - 1], kx_recv.at[source, i - 1], x_peer(i), head
        )

    def kv_x_in(source, i):
        slot = kvbuf.at[source * nx + lax.rem(x + nx - i, nx)]
        return remote(
            slot, slot, kx_send.at[source, i - 1], kx_recv.at[source, i - 1], x_peer(nx - i), head
        )

    def along_z(distances, act):
        for d in distances:

            @pl.when(z + d < nz)
            def _():
                act(z + d)

            @pl.when(z - d >= 0)
            def _():
                act(z - d)

    def kv_forward(distances):
        def pass_on(source):
            kv_z_in(source).wait_recv()
            for i in range(1, nx):
                kv_x(source, i, False).start()

        along_z(distances, pass_on)

    def part_core(b, j):
        return remote(
            psend.at[b, j], precv.at[b, j], p_send.at[b, j], p_recv.at[b, j], seq, partner
        )

    def part_y(b, j):
        return remote(
            ysend.at[b, j - 1],
            yrecv.at[b, j - 1],
            r_send.at[b, j - 1],
            r_recv.at[b, j - 1],
            seq,
            y_peer(j),
        )

    def send_tokens(b):
        for j in range(1, ny):
            tok_y(b, j).start()

    own_copy().start()
    for i in range(3):
        weight_copy(i, 0).start()

    lane = lax.broadcasted_iota(jnp.int32, (BLOCK_TOKENS, BLOCK_TOKENS), 1)
    row = lax.broadcasted_iota(jnp.int32, (BLOCK_TOKENS, BLOCK_TOKENS), 0)
    identity = jnp.where(lane == row, 1.0, 0.0).astype(jnp.bfloat16)
    causal = jnp.where(row <= lane, 0.0, MASKED).astype(jnp.bfloat16)

    def fill(b, carry):
        for k in range(q_cols // HEAD_SIZE):
            qbuf[b, k, :, HEAD_SIZE:] = identity
        return carry

    lax.fori_loop(0, blocks, fill, 0)
    for g in range(kv_heads):
        kcat[g, DEPTH * BLOCK_TOKENS :, HEAD_SIZE:] = causal
        vcat[g, :, HEAD_SIZE:] = jnp.ones((KEYS, HEAD_SIZE), jnp.bfloat16)

    pl.semaphore_wait(barrier, len(peers))
    tok_core().start()
    send_tokens(0)
    for j in range(1, ny):
        for i in range(3):
            weight_copy(i, j).start()

    def angles(b, carry):
        base = vis_ref[b, 0]
        for j in range(1, DEPTH):
            base += vis_ref[b, j]
        angle = (base + row).astype(jnp.float32) * freq_ref[...]
        cosine[b] = jnp.cos(angle)
        turn = jnp.sin(angle)
        sine[b] = jnp.where(lane < HEAD_SIZE // 2, -turn, turn)
        return carry

    lax.fori_loop(0, blocks, angles, 0)

    def scale_rows(b, j):
        total = jnp.zeros((BLOCK_TOKENS, 1), jnp.float32)
        for c in range(2):
            piece = xbuf[j, c, block_rows(b)].astype(jnp.float32)
            first = (2 * lax.rem(y + j, ny) + c) * width
            gain = gain_ref[:, pl.ds(pl.multiple_of(first, width), width)]
            scaled[block_rows(b), c * width : (c + 1) * width] = (piece * gain).astype(jnp.bfloat16)
            total += jnp.sum(piece * piece, axis=1, keepdims=True)
        return jnp.broadcast_to(total, (BLOCK_TOKENS, HEAD_SIZE))

    own_copy().wait()
    tok_core_in().wait_recv()

    def scale_own(b, carry):
        square[b] = scale_rows(b, 0)
        return carry

    lax.fori_loop(0, blocks, scale_own, 0)
    for i in range(3):
        weight_copy(i, 0).wait()
    part[:, q_cols : q_cols + kv_cols] = jnp.dot(
        scaled[...], wk[0], preferred_element_type=jnp.float32
    )
    part[:, q_cols + kv_cols :] = jnp.dot(scaled[...], wv[0], preferred_element_type=jnp.float32)
    tile = 2 * HEAD_SIZE

    def own_tile(t, carry):
        cols = pl.ds(pl.multiple_of(t * tile, tile), tile)
        part[:, cols] = jnp.dot(scaled[...], wq[0, :, cols], preferred_element_type=jnp.float32)
        return carry

    lax.fori_loop(0, q_cols // tile, own_tile, 0)

    def project(b, carry):
        for j in range(1, ny):
            tok_y(b, j).wait_recv()
            tok_fwd(b, j).start()

        @pl.when(b < blocks - 1)
        def _():
            send_tokens(b + 1)

        @pl.when(b == 0)
        def _():
            out_copy().start()
            for j in range(1, ny):
                for i in range(3):
                    weight_copy(i, j).wait()

        rows_b = block_rows(b)

        def add_far(first, weight, cols, j):
            into = (rows_b, pl.ds(first, cols))
            part[into] += jnp.dot(scaled[rows_b], weight, preferred_element_type=jnp.float32)

        for j in range(1, ny):
            tok_fwd_in(b, j).wait_recv()
            square[b] += scale_rows(b, j)
            add_far(q_cols, wk[j], kv_cols, j)
            add_far(q_cols + kv_cols, wv[j], kv_cols, j)
            if j < ny - 1:

                def far_tile(t, inner):
                    first = pl.multiple_of(t * tile, tile)
                    add_far(first, wq[j, :, pl.ds(first, tile)], tile, j)
                    return inner

                lax.fori_loop(0, q_cols // tile, far_tile, 0)
        scale = lax.rsqrt(square[b] / (n_head * width) + NORM_EPS)

        def rope(vectors):
            vectors = vectors * scale
            return vectors * cosine[b] + pltpu.roll(vectors, HEAD_SIZE // 2, 1) * sine[b]

        for g in range(kv_heads):
            cols = slice(g * HEAD_SIZE, (g + 1) * HEAD_SIZE)
            at = q_cols + g * HEAD_SIZE
            kvbuf[n_seq + b, :, cols] = rope(part[rows_b, at : at + HEAD_SIZE]).astype(jnp.bfloat16)
            at += kv_cols
            cols = slice(kv_cols + g * HEAD_SIZE, kv_cols + (g + 1) * HEAD_SIZE)
            kvbuf[n_seq + b, :, cols] = (part[rows_b, at : at + HEAD_SIZE] * scale).astype(
                jnp.bfloat16
            )

        @pl.when(b == 0)
        def _():
            for i in range(1, nx):
                kv_x(z, i, True).start()
            along_z(range(1, nz), lambda to: kv_z(to).start())

        def query_tile(t, inner):
            first = pl.multiple_of(t * tile, tile)
            cols = pl.ds(first, tile)
            found = part[rows_b, cols] + jnp.dot(
                scaled[rows_b], wq[ny - 1, :, cols], preferred_element_type=jnp.float32
            )
            for k in range(2):
                turned = rope(found[:, k * HEAD_SIZE : (k + 1) * HEAD_SIZE])
                qbuf[b, 2 * t + k, :, :HEAD_SIZE] = (turned * (HEAD_SIZE**-0.5 * LOG2E)).astype(
                    jnp.bfloat16
                )
            return inner

        lax.fori_loop(0, q_cols // tile, query_tile, 0)

        @pl.when(b == 1)
        def _():
            kv_forward(range(1, 2))

        @pl.when(b == 2)
        def _():
            kv_forward(range(2, nz))

        return carry

    lax.fori_loop(0, blocks, project, 0)

    out_copy().wait()
    for source in range(nz):
        for i in range(1, nx):
            kv_x_in(source, i).wait_recv()

    def attend(b, carry):
        for j in range(SLOTS):
            span = slice(j * BLOCK_TOKENS, (j + 1) * BLOCK_TOKENS)
            if j < DEPTH:
                block_id = jnp.maximum(anc_ref[b, j], 0)
                owner, inside = lax.div(block_id, blocks), lax.rem(block_id, blocks)
                slot = jnp.where(owner == seq, n_seq + inside, owner)
                mask = jnp.where(row < vis_ref[b, j], 0.0, MASKED).astype(jnp.bfloat16)
            else:
                slot = n_seq + b
            for g in range(kv_heads):
                cols = slice(g * HEAD_SIZE, (g + 1) * HEAD_SIZE)
                kcat[g, span, :HEAD_SIZE] = kvbuf[slot, :, cols]
                cols = slice(kv_cols + g * HEAD_SIZE, kv_cols + (g + 1) * HEAD_SIZE)
                vcat[g, span, :HEAD_SIZE] = kvbuf[slot, :, cols]
                if j < DEPTH:
                    kcat[g, span, HEAD_SIZE:] = mask

        for g in range(kv_heads):
            query = qbuf[b, g * group : (g + 1) * group].reshape(
                group * BLOCK_TOKENS, 2 * HEAD_SIZE
            )
            scores = lax.dot_general(
                query, kcat[g], (((1,), (1,)), ((), ())), preferred_element_type=jnp.float32
            )
            top = jnp.max(scores, axis=1, keepdims=True)
            weight = jnp.exp2(scores - top).astype(jnp.bfloat16)
            mixed = jnp.dot(weight, vcat[g], preferred_element_type=jnp.float32)
            mixed = (mixed[:, :HEAD_SIZE] / mixed[:, HEAD_SIZE:]).astype(jnp.bfloat16)
            for k in range(group):
                at = (g * group + k) * HEAD_SIZE
                attn[:, at : at + HEAD_SIZE] = mixed[k * BLOCK_TOKENS : (k + 1) * BLOCK_TOKENS]

        tile = 512

        def share(j, side, store):
            base = (2 * lax.rem(y + j, ny) + side) * width

            def one_tile(t, inner):
                cols = pl.ds(pl.multiple_of(base + t * tile, tile), tile)
                into = pl.ds(pl.multiple_of(t * tile, tile), tile)
                store(into, jnp.dot(attn[...], wo[:, cols], preferred_element_type=jnp.float32))
                return inner

            lax.fori_loop(0, width // tile, one_tile, 0)

        def other_share(j):
            def store(into, found):
                psend[b, j, :, into] = found.astype(jnp.bfloat16)

            share(j, 1 - core, store)
            part_core(b, j).start()

        for j in range(1, ny):
            other_share(j)
        for j in range(1, ny):

            def add(into, found):
                acc[b, :, into] = found

            share(j, core, add)
            part_core(b, j).wait_recv()
            ysend[b, j - 1] = (acc[b] + precv[b, j].astype(jnp.float32)).astype(jnp.bfloat16)
            part_y(b, j).start()
        other_share(0)

        def keep(into, found):
            acc[b, :, into] = found

        share(0, core, keep)
        return carry

    lax.fori_loop(0, blocks, attend, 0)

    def finish(b, carry):
        part_core(b, 0).wait_recv()
        result = acc[b] + precv[b, 0].astype(jnp.float32)
        for j in range(1, ny):
            part_y(b, j).wait_recv()
            result += yrecv[b, j - 1].astype(jnp.float32)
        out_ref[pl.ds(pl.multiple_of(b * BLOCK_TOKENS, BLOCK_TOKENS), BLOCK_TOKENS)] = (
            result.astype(jnp.bfloat16)
        )
        for j in range(1, ny):
            tok_y(b, j).wait_send()
            tok_fwd(b, j).wait_send()
            part_y(b, j).wait_send()
        for j in range(ny):
            part_core(b, j).wait_send()
        return carry

    lax.fori_loop(0, blocks, finish, 0)
    tok_core().wait_send()
    along_z(range(1, nz), lambda to: kv_z(to).wait_send())
    for source in range(nz):
        for i in range(1, nx):
            kv_x(source, i, True).wait_send()


def local(
    n_seq,
    n_head,
    tokens,
    norm_gain,
    w_query,
    key_weight,
    value_weight,
    w_out,
    ancestor_blocks,
    visible_counts,
):
    rows, width = tokens.shape
    blocks = rows // BLOCK_TOKENS
    q_cols = w_query.shape[1]
    kv_cols = key_weight.shape[1]
    ny = n_head // 2
    nx = ny
    nz = n_seq // nx
    half = HEAD_SIZE // 2
    frequency = ROPE_BASE ** (-(np.arange(half) * 2.0) / HEAD_SIZE)
    frequency = np.concatenate([frequency, frequency]).astype(np.float32)[None]
    dma = pltpu.SemaphoreType.DMA
    vmem = pl.BlockSpec(memory_space=pltpu.VMEM)
    smem = pl.BlockSpec(memory_space=pltpu.SMEM)
    hbm = pl.BlockSpec(memory_space=pl.ANY)
    bf16, f32 = jnp.bfloat16, jnp.float32
    return pl.pallas_call(
        functools.partial(kernel, n_seq, n_head),
        out_shape=jax.ShapeDtypeStruct((rows, width), bf16),
        in_specs=[hbm, vmem, vmem, hbm, hbm, hbm, hbm, smem, smem],
        out_specs=vmem,
        scratch_shapes=[
            pltpu.VMEM((ny, 2, rows, width), bf16),
            pltpu.VMEM((ny, 2 * width, q_cols), bf16),
            pltpu.VMEM((ny, 2 * width, kv_cols), bf16),
            pltpu.VMEM((ny, 2 * width, kv_cols), bf16),
            pltpu.VMEM(w_out.shape, bf16),
            pltpu.VMEM((rows, 2 * width), bf16),
            pltpu.VMEM((rows, q_cols + 2 * kv_cols), f32),
            pltpu.VMEM((blocks, BLOCK_TOKENS, HEAD_SIZE), f32),
            pltpu.VMEM((blocks, BLOCK_TOKENS, HEAD_SIZE), f32),
            pltpu.VMEM((blocks, BLOCK_TOKENS, HEAD_SIZE), f32),
            pltpu.VMEM((blocks, q_cols // HEAD_SIZE, BLOCK_TOKENS, 2 * HEAD_SIZE), bf16),
            pltpu.VMEM((n_seq + blocks, BLOCK_TOKENS, 2 * kv_cols), bf16),
            pltpu.VMEM((kv_cols // HEAD_SIZE, KEYS, 2 * HEAD_SIZE), bf16),
            pltpu.VMEM((kv_cols // HEAD_SIZE, KEYS, 2 * HEAD_SIZE), bf16),
            pltpu.VMEM((BLOCK_TOKENS, q_cols), bf16),
            pltpu.VMEM((blocks, ny, BLOCK_TOKENS, width), bf16),
            pltpu.VMEM((blocks, ny, BLOCK_TOKENS, width), bf16),
            pltpu.VMEM((blocks, BLOCK_TOKENS, width), f32),
            pltpu.VMEM((blocks, ny - 1, BLOCK_TOKENS, width), bf16),
            pltpu.VMEM((blocks, ny - 1, BLOCK_TOKENS, width), bf16),
            dma((3, ny)),
            dma,
            dma,
            dma((blocks, ny - 1)),
            dma((blocks, ny - 1)),
            dma,
            dma,
            dma((blocks, ny - 1)),
            dma((blocks, ny - 1)),
            dma((nz,)),
            dma((nz,)),
            dma((nz, nx - 1)),
            dma((nz, nx - 1)),
            dma((blocks, ny)),
            dma((blocks, ny)),
            dma((blocks, ny - 1)),
            dma((blocks, ny - 1)),
        ],
        compiler_params=pltpu.CompilerParams(
            collective_id=0, has_side_effects=True, vmem_limit_bytes=60 * 1024 * 1024
        ),
        cost_estimate=pl.CostEstimate(
            flops=13 * 10**9, bytes_accessed=25 * 10**6, transcendentals=5 * 10**6
        ),
    )(
        tokens,
        norm_gain[None],
        jnp.asarray(frequency),
        w_query,
        key_weight,
        value_weight,
        w_out,
        ancestor_blocks,
        visible_counts,
    )


def solution(mesh):
    placed = (
        P("seq", "head"),
        P(),
        P(None, "head"),
        P(None, "head"),
        P(None, "head"),
        P("head", None),
        P("seq", None),
        P("seq", None),
    )
    return jax.shard_map(
        functools.partial(local, mesh.shape["seq"], mesh.shape["head"]),
        mesh=mesh,
        in_specs=placed,
        out_specs=P("seq", "head"),
        check_vma=False,
    )
```

```python
import functools

import numpy as np

import jax
import jax.numpy as jnp
from jax import lax
from jax.experimental import pallas as pl
from jax.experimental.pallas import tpu as pltpu
from jax.sharding import PartitionSpec as P

HEAD_SIZE = 128
BLOCK_TOKENS = 128
DEPTH = 8
ROPE_BASE = 500000.0
NORM_EPS = 1e-05
MESH = pl.DeviceIdType.MESH
SLOTS = DEPTH + 1
KEYS = SLOTS * BLOCK_TOKENS
LOG2E = 1.4426950408889634
MASKED = -1e30


def kernel(
    n_seq,
    n_head,
    tok_ref,
    gain_ref,
    freq_ref,
    wq_ref,
    wk_ref,
    wv_ref,
    wo_ref,
    anc_ref,
    vis_ref,
    out_ref,
    xbuf,
    wq,
    wk,
    wv,
    wo,
    scaled,
    far,
    part,
    square,
    cosine,
    sine,
    qbuf,
    kvbuf,
    kcat,
    vcat,
    attn,
    psend,
    precv,
    acc,
    ysend,
    yrecv,
    w_sem,
    o_sem,
    own_sem,
    ty_send,
    ty_recv,
    tc_send,
    tc_recv,
    tf_send,
    tf_recv,
    kz_send,
    kz_recv,
    kx_send,
    kx_recv,
    p_send,
    p_recv,
    r_send,
    r_recv,
):
    rows, width = tok_ref.shape
    blocks = rows // BLOCK_TOKENS
    q_cols = wq.shape[2]
    kv_cols = wk.shape[2]
    kv_heads = kv_cols // HEAD_SIZE
    group = q_cols // kv_cols
    ny = n_head // 2
    nx = ny
    nz = n_seq // nx
    seq = lax.axis_index("seq")
    head = lax.axis_index("head")
    y, core = lax.div(head, 2), lax.rem(head, 2)
    z, x = lax.div(seq, nx), lax.rem(seq, nx)
    partner = 2 * y + 1 - core

    def y_peer(j):
        return 2 * lax.rem(y + j, ny) + core

    def z_peer(j):
        return lax.rem(z + j, nz) * nx + x

    def x_peer(i):
        return z * nx + lax.rem(x + i, nx)

    def remote(src, dst, send, recv, seq_id, head_id):
        return pltpu.make_async_remote_copy(
            src_ref=src,
            dst_ref=dst,
            send_sem=send,
            recv_sem=recv,
            device_id=(seq_id, head_id),
            device_id_type=MESH,
        )

    barrier = pltpu.get_barrier_semaphore()
    peers = [(seq, partner)]
    peers += [(seq, y_peer(j)) for j in range(1, ny)]
    peers += [(z_peer(j), head) for j in range(1, nz)]
    peers += [(x_peer(i), head) for i in range(1, nx)]
    for peer in peers:
        pl.semaphore_signal(barrier, inc=1, device_id=peer, device_id_type=MESH)

    def weight_copy(i, j):
        source = (wk_ref, wv_ref, wq_ref)[i]
        first = pl.multiple_of(2 * width * lax.rem(y + j, ny), 2 * width)
        return pltpu.make_async_copy(
            source.at[pl.ds(first, 2 * width)], (wk, wv, wq)[i].at[j], w_sem.at[i, j]
        )

    def out_copy():
        return pltpu.make_async_copy(wo_ref, wo, o_sem)

    def block_rows(b):
        return pl.ds(pl.multiple_of(b * BLOCK_TOKENS, BLOCK_TOKENS), BLOCK_TOKENS)

    def own_copy():
        return pltpu.make_async_copy(tok_ref, xbuf.at[0, core], own_sem)

    def tok_y(b, j):
        return remote(
            tok_ref.at[block_rows(b)],
            xbuf.at[ny - j, core, block_rows(b)],
            ty_send.at[b, j - 1],
            ty_recv.at[b, j - 1],
            seq,
            y_peer(j),
        )

    def tok_core():
        return remote(tok_ref, xbuf.at[0, core], tc_send, tc_recv, seq, partner)

    def tok_core_in():
        slot = xbuf.at[0, 1 - core]
        return remote(slot, slot, tc_send, tc_recv, seq, partner)

    def tok_fwd(b, j):
        slot = xbuf.at[ny - j, core, block_rows(b)]
        return remote(slot, slot, tf_send.at[b, j - 1], tf_recv.at[b, j - 1], seq, partner)

    def tok_fwd_in(b, j):
        slot = xbuf.at[ny - j, 1 - core, block_rows(b)]
        return remote(slot, slot, tf_send.at[b, j - 1], tf_recv.at[b, j - 1], seq, partner)

    def kv_z(to):
        return remote(
            kvbuf.at[n_seq], kvbuf.at[seq], kz_send.at[to], kz_recv.at[z], to * nx + x, head
        )

    def kv_z_in(source):
        slot = kvbuf.at[source * nx + x]
        return remote(slot, slot, kz_send.at[source], kz_recv.at[source], source * nx + x, head)

    def kv_x(source, i, own):
        slot = kvbuf.at[source * nx + x]
        src = kvbuf.at[n_seq] if own else slot
        return remote(
            src, slot, kx_send.at[source, i - 1], kx_recv.at[source, i - 1], x_peer(i), head
        )

    def kv_x_in(source, i):
        slot = kvbuf.at[source * nx + lax.rem(x + nx - i, nx)]
        return remote(
            slot, slot, kx_send.at[source, i - 1], kx_recv.at[source, i - 1], x_peer(nx - i), head
        )

    def along_z(distances, act):
        for d in distances:

            @pl.when(z + d < nz)
            def _():
                act(z + d)

            @pl.when(z - d >= 0)
            def _():
                act(z - d)

    def kv_forward(distances):
        def pass_on(source):
            kv_z_in(source).wait_recv()
            for i in range(1, nx):
                kv_x(source, i, False).start()

        along_z(distances, pass_on)

    def part_core(b, j):
        return remote(
            psend.at[b, j], precv.at[b, j], p_send.at[b, j], p_recv.at[b, j], seq, partner
        )

    def part_y(b, j):
        return remote(
            ysend.at[b, j - 1],
            yrecv.at[b, j - 1],
            r_send.at[b, j - 1],
            r_recv.at[b, j - 1],
            seq,
            y_peer(j),
        )

    def send_tokens(b):
        for j in range(1, ny):
            tok_y(b, j).start()

    own_copy().start()
    for i in range(3):
        weight_copy(i, 0).start()

    lane = lax.broadcasted_iota(jnp.int32, (BLOCK_TOKENS, BLOCK_TOKENS), 1)
    row = lax.broadcasted_iota(jnp.int32, (BLOCK_TOKENS, BLOCK_TOKENS), 0)
    identity = jnp.where(lane == row, 1.0, 0.0).astype(jnp.bfloat16)
    causal = jnp.where(row <= lane, 0.0, MASKED).astype(jnp.bfloat16)

    def fill(b, carry):
        for k in range(q_cols // HEAD_SIZE):
            qbuf[b, k, :, HEAD_SIZE:] = identity
        return carry

    lax.fori_loop(0, blocks, fill, 0)
    for g in range(kv_heads):
        kcat[g, DEPTH * BLOCK_TOKENS :, HEAD_SIZE:] = causal
        vcat[g, :, HEAD_SIZE:] = jnp.ones((KEYS, HEAD_SIZE), jnp.bfloat16)

    pl.semaphore_wait(barrier, len(peers))
    send_tokens(0)
    tok_core().start()
    send_tokens(1)
    for j in range(1, ny):
        for i in range(3):
            weight_copy(i, j).start()

    def angles(b, carry):
        base = vis_ref[b, 0]
        for j in range(1, DEPTH):
            base += vis_ref[b, j]
        angle = (base + row).astype(jnp.float32) * freq_ref[...]
        cosine[b] = jnp.cos(angle)
        turn = jnp.sin(angle)
        sine[b] = jnp.where(lane < HEAD_SIZE // 2, -turn, turn)
        return carry

    lax.fori_loop(0, blocks, angles, 0)

    def scale_rows(b, j, into, into_rows):
        total = jnp.zeros((BLOCK_TOKENS, 1), jnp.float32)
        for c in range(2):
            piece = xbuf[j, c, block_rows(b)].astype(jnp.float32)
            first = (2 * lax.rem(y + j, ny) + c) * width
            gain = gain_ref[:, pl.ds(pl.multiple_of(first, width), width)]
            at = (max(j - 1, 0) * 2 + c) * width
            into[into_rows, at : at + width] = (piece * gain).astype(jnp.bfloat16)
            total += jnp.sum(piece * piece, axis=1, keepdims=True)
        return jnp.broadcast_to(total, (BLOCK_TOKENS, HEAD_SIZE))

    own_copy().wait()
    tok_core_in().wait_recv()

    def scale_own(b, carry):
        square[b] = scale_rows(b, 0, scaled, block_rows(b))
        return carry

    lax.fori_loop(0, blocks, scale_own, 0)
    for i in range(2):
        weight_copy(i, 0).wait()
    part[:, q_cols : q_cols + kv_cols] = jnp.dot(
        scaled[...], wk[0], preferred_element_type=jnp.float32
    )
    part[:, q_cols + kv_cols :] = jnp.dot(scaled[...], wv[0], preferred_element_type=jnp.float32)
    tile = 2 * HEAD_SIZE

    def own_tile(t, carry):
        cols = pl.ds(pl.multiple_of(t * tile, tile), tile)
        part[:, cols] = jnp.dot(scaled[...], wq[0, :, cols], preferred_element_type=jnp.float32)
        return carry

    def arrive(b):
        for j in range(1, ny):
            tok_y(b, j).wait_recv()
            tok_fwd(b, j).start()

        @pl.when(b < blocks - 2)
        def _():
            send_tokens(b + 2)

        @pl.when(b == 0)
        def _():
            out_copy().start()
            for j in range(1, ny):
                for i in range(2):
                    weight_copy(i, j).wait()

        rows_b = block_rows(b)

        def add_far(first, weight, cols, j):
            into = (rows_b, pl.ds(first, cols))
            part[into] += jnp.dot(far[:, (j - 1) * 2 * width : j * 2 * width], weight, preferred_element_type=jnp.float32)

        for j in range(1, ny):
            tok_fwd_in(b, j).wait_recv()
            square[b] += scale_rows(b, j, far, slice(None))
            add_far(q_cols, wk[j], kv_cols, j)
            add_far(q_cols + kv_cols, wv[j], kv_cols, j)
        scale = lax.rsqrt(square[b] / (n_head * width) + NORM_EPS)

        def rope(vectors):
            vectors = vectors * scale
            return vectors * cosine[b] + pltpu.roll(vectors, HEAD_SIZE // 2, 1) * sine[b]

        for g in range(kv_heads):
            cols = slice(g * HEAD_SIZE, (g + 1) * HEAD_SIZE)
            at = q_cols + g * HEAD_SIZE
            kvbuf[n_seq + b, :, cols] = rope(part[rows_b, at : at + HEAD_SIZE]).astype(jnp.bfloat16)
            at += kv_cols
            cols = slice(kv_cols + g * HEAD_SIZE, kv_cols + (g + 1) * HEAD_SIZE)
            kvbuf[n_seq + b, :, cols] = (part[rows_b, at : at + HEAD_SIZE] * scale).astype(
                jnp.bfloat16
            )

        @pl.when(b == 0)
        def _():
            for i in range(1, nx):
                kv_x(z, i, True).start()
            along_z(range(1, nz), lambda to: kv_z(to).start())
            for j in range(ny):
                weight_copy(2, j).wait()
            lax.fori_loop(0, q_cols // tile, own_tile, 0)

        def query_tile(t, inner):
            first = pl.multiple_of(t * tile, tile)
            cols = pl.ds(first, tile)
            found = part[rows_b, cols]
            for j in range(1, ny):
                found += jnp.dot(
                    far[:, (j - 1) * 2 * width : j * 2 * width],
                    wq[j, :, cols],
                    preferred_element_type=jnp.float32,
                )
            for k in range(2):
                turned = rope(found[:, k * HEAD_SIZE : (k + 1) * HEAD_SIZE])
                qbuf[b, 2 * t + k, :, :HEAD_SIZE] = (turned * (HEAD_SIZE**-0.5 * LOG2E)).astype(
                    jnp.bfloat16
                )
            return inner

        lax.fori_loop(0, q_cols // tile, query_tile, 0)

        for stage, distances in enumerate(((1,), (2,), range(3, nz))):

            @pl.when(b == stage)
            def _():
                kv_forward([d for d in distances if d < nz])

    def attend(b):
        for j in range(SLOTS):
            span = slice(j * BLOCK_TOKENS, (j + 1) * BLOCK_TOKENS)
            if j < DEPTH:
                block_id = jnp.maximum(anc_ref[b, j], 0)
                owner, inside = lax.div(block_id, blocks), lax.rem(block_id, blocks)
                slot = jnp.where(owner == seq, n_seq + inside, owner)
                mask = jnp.where(row < vis_ref[b, j], 0.0, MASKED).astype(jnp.bfloat16)
            else:
                slot = n_seq + b
            for g in range(kv_heads):
                cols = slice(g * HEAD_SIZE, (g + 1) * HEAD_SIZE)
                kcat[g, span, :HEAD_SIZE] = kvbuf[slot, :, cols]
                cols = slice(kv_cols + g * HEAD_SIZE, kv_cols + (g + 1) * HEAD_SIZE)
                vcat[g, span, :HEAD_SIZE] = kvbuf[slot, :, cols]
                if j < DEPTH:
                    kcat[g, span, HEAD_SIZE:] = mask

        for g in range(kv_heads):
            query = qbuf[b, g * group : (g + 1) * group].reshape(
                group * BLOCK_TOKENS, 2 * HEAD_SIZE
            )
            scores = lax.dot_general(
                query, kcat[g], (((1,), (1,)), ((), ())), preferred_element_type=jnp.float32
            )
            top = jnp.max(scores, axis=1, keepdims=True)
            weight = jnp.exp2(scores - top).astype(jnp.bfloat16)
            mixed = jnp.dot(weight, vcat[g], preferred_element_type=jnp.float32)
            mixed = (mixed[:, :HEAD_SIZE] / mixed[:, HEAD_SIZE:]).astype(jnp.bfloat16)
            for k in range(group):
                at = (g * group + k) * HEAD_SIZE
                attn[:, at : at + HEAD_SIZE] = mixed[k * BLOCK_TOKENS : (k + 1) * BLOCK_TOKENS]

        tile = 512

        def share(j, side, store):
            base = (2 * lax.rem(y + j, ny) + side) * width

            def one_tile(t, inner):
                cols = pl.ds(pl.multiple_of(base + t * tile, tile), tile)
                into = pl.ds(pl.multiple_of(t * tile, tile), tile)
                store(into, jnp.dot(attn[...], wo[:, cols], preferred_element_type=jnp.float32))
                return inner

            lax.fori_loop(0, width // tile, one_tile, 0)

        def other_share(j):
            def store(into, found):
                psend[b, j, :, into] = found.astype(jnp.bfloat16)

            share(j, 1 - core, store)
            part_core(b, j).start()

        for j in range(1, ny):
            other_share(j)
        for j in range(1, ny):

            def add(into, found):
                acc[b, :, into] = found

            share(j, core, add)
            part_core(b, j).wait_recv()
            ysend[b, j - 1] = (acc[b] + precv[b, j].astype(jnp.float32)).astype(jnp.bfloat16)
            part_y(b, j).start()
        other_share(0)

        def keep(into, found):
            acc[b, :, into] = found

        share(0, core, keep)

    lag = 2

    def step(s, carry):
        @pl.when(s < blocks)
        def _():
            arrive(s)

        @pl.when(s == lag)
        def _():
            out_copy().wait()
            for source in range(nz):
                for i in range(1, nx):
                    kv_x_in(source, i).wait_recv()

        @pl.when(s >= lag)
        def _():
            attend(s - lag)

        return carry

    lax.fori_loop(0, blocks + lag, step, 0)

    def finish(b, carry):
        part_core(b, 0).wait_recv()
        result = acc[b] + precv[b, 0].astype(jnp.float32)
        for j in range(1, ny):
            part_y(b, j).wait_recv()
            result += yrecv[b, j - 1].astype(jnp.float32)
        out_ref[pl.ds(pl.multiple_of(b * BLOCK_TOKENS, BLOCK_TOKENS), BLOCK_TOKENS)] = (
            result.astype(jnp.bfloat16)
        )
        for j in range(1, ny):
            tok_y(b, j).wait_send()
            tok_fwd(b, j).wait_send()
            part_y(b, j).wait_send()
        for j in range(ny):
            part_core(b, j).wait_send()
        return carry

    lax.fori_loop(0, blocks, finish, 0)
    tok_core().wait_send()
    along_z(range(1, nz), lambda to: kv_z(to).wait_send())
    for source in range(nz):
        for i in range(1, nx):
            kv_x(source, i, True).wait_send()


def local(
    n_seq,
    n_head,
    tokens,
    norm_gain,
    w_query,
    key_weight,
    value_weight,
    w_out,
    ancestor_blocks,
    visible_counts,
):
    rows, width = tokens.shape
    blocks = rows // BLOCK_TOKENS
    q_cols = w_query.shape[1]
    kv_cols = key_weight.shape[1]
    ny = n_head // 2
    nx = ny
    nz = n_seq // nx
    half = HEAD_SIZE // 2
    frequency = ROPE_BASE ** (-(np.arange(half) * 2.0) / HEAD_SIZE)
    frequency = np.concatenate([frequency, frequency]).astype(np.float32)[None]
    dma = pltpu.SemaphoreType.DMA
    vmem = pl.BlockSpec(memory_space=pltpu.VMEM)
    smem = pl.BlockSpec(memory_space=pltpu.SMEM)
    hbm = pl.BlockSpec(memory_space=pl.ANY)
    bf16, f32 = jnp.bfloat16, jnp.float32
    return pl.pallas_call(
        functools.partial(kernel, n_seq, n_head),
        out_shape=jax.ShapeDtypeStruct((rows, width), bf16),
        in_specs=[hbm, vmem, vmem, hbm, hbm, hbm, hbm, smem, smem],
        out_specs=vmem,
        scratch_shapes=[
            pltpu.VMEM((ny, 2, rows, width), bf16),
            pltpu.VMEM((ny, 2 * width, q_cols), bf16),
            pltpu.VMEM((ny, 2 * width, kv_cols), bf16),
            pltpu.VMEM((ny, 2 * width, kv_cols), bf16),
            pltpu.VMEM(w_out.shape, bf16),
            pltpu.VMEM((rows, 2 * width), bf16),
            pltpu.VMEM((BLOCK_TOKENS, (ny - 1) * 2 * width), bf16),
            pltpu.VMEM((rows, q_cols + 2 * kv_cols), f32),
            pltpu.VMEM((blocks, BLOCK_TOKENS, HEAD_SIZE), f32),
            pltpu.VMEM((blocks, BLOCK_TOKENS, HEAD_SIZE), f32),
            pltpu.VMEM((blocks, BLOCK_TOKENS, HEAD_SIZE), f32),
            pltpu.VMEM((blocks, q_cols // HEAD_SIZE, BLOCK_TOKENS, 2 * HEAD_SIZE), bf16),
            pltpu.VMEM((n_seq + blocks, BLOCK_TOKENS, 2 * kv_cols), bf16),
            pltpu.VMEM((kv_cols // HEAD_SIZE, KEYS, 2 * HEAD_SIZE), bf16),
            pltpu.VMEM((kv_cols // HEAD_SIZE, KEYS, 2 * HEAD_SIZE), bf16),
            pltpu.VMEM((BLOCK_TOKENS, q_cols), bf16),
            pltpu.VMEM((blocks, ny, BLOCK_TOKENS, width), bf16),
            pltpu.VMEM((blocks, ny, BLOCK_TOKENS, width), bf16),
            pltpu.VMEM((blocks, BLOCK_TOKENS, width), f32),
            pltpu.VMEM((blocks, ny - 1, BLOCK_TOKENS, width), bf16),
            pltpu.VMEM((blocks, ny - 1, BLOCK_TOKENS, width), bf16),
            dma((3, ny)),
            dma,
            dma,
            dma((blocks, ny - 1)),
            dma((blocks, ny - 1)),
            dma,
            dma,
            dma((blocks, ny - 1)),
            dma((blocks, ny - 1)),
            dma((nz,)),
            dma((nz,)),
            dma((nz, nx - 1)),
            dma((nz, nx - 1)),
            dma((blocks, ny)),
            dma((blocks, ny)),
            dma((blocks, ny - 1)),
            dma((blocks, ny - 1)),
        ],
        compiler_params=pltpu.CompilerParams(
            collective_id=0, has_side_effects=True, vmem_limit_bytes=60 * 1024 * 1024
        ),
        cost_estimate=pl.CostEstimate(
            flops=13 * 10**9, bytes_accessed=25 * 10**6, transcendentals=5 * 10**6
        ),
    )(
        tokens,
        norm_gain[None],
        jnp.asarray(frequency),
        w_query,
        key_weight,
        value_weight,
        w_out,
        ancestor_blocks,
        visible_counts,
    )


def solution(mesh):
    placed = (
        P("seq", "head"),
        P(),
        P(None, "head"),
        P(None, "head"),
        P(None, "head"),
        P("head", None),
        P("seq", None),
        P("seq", None),
    )
    return jax.shard_map(
        functools.partial(local, mesh.shape["seq"], mesh.shape["head"]),
        mesh=mesh,
        in_specs=placed,
        out_specs=P("seq", "head"),
        check_vma=False,
    )
```

```python
import functools

import numpy as np

import jax
import jax.numpy as jnp
from jax import lax
from jax.experimental import pallas as pl
from jax.experimental.pallas import tpu as pltpu
from jax.sharding import PartitionSpec as P

HEAD_SIZE = 128
BLOCK_TOKENS = 128
DEPTH = 8
ROPE_BASE = 500000.0
NORM_EPS = 1e-05
MESH = pl.DeviceIdType.MESH
SLOTS = DEPTH + 1
KEYS = SLOTS * BLOCK_TOKENS
LOG2E = 1.4426950408889634
MASKED = -1e30


def kernel(
    n_seq,
    n_head,
    tok_ref,
    gain_ref,
    freq_ref,
    wq_ref,
    wk_ref,
    wv_ref,
    wo_ref,
    anc_ref,
    vis_ref,
    out_ref,
    xbuf,
    wq,
    wk,
    wv,
    wo,
    scaled,
    far,
    part,
    square,
    cosine,
    sine,
    qbuf,
    kvbuf,
    kcat,
    vcat,
    attn,
    psend,
    precv,
    far_sum,
    acc,
    ysend,
    yrecv,
    w_sem,
    o_sem,
    own_sem,
    ty_send,
    ty_recv,
    tc_send,
    tc_recv,
    tf_send,
    tf_recv,
    kz_send,
    kz_recv,
    kx_send,
    kx_recv,
    p_send,
    p_recv,
    r_send,
    r_recv,
):
    rows, width = tok_ref.shape
    blocks = rows // BLOCK_TOKENS
    q_cols = wq.shape[2]
    kv_cols = wk.shape[2]
    kv_heads = kv_cols // HEAD_SIZE
    group = q_cols // kv_cols
    ny = n_head // 2
    nx = ny
    nz = n_seq // nx
    seq = lax.axis_index("seq")
    head = lax.axis_index("head")
    y, core = lax.div(head, 2), lax.rem(head, 2)
    z, x = lax.div(seq, nx), lax.rem(seq, nx)
    partner = 2 * y + 1 - core

    def y_peer(j):
        return 2 * lax.rem(y + j, ny) + core

    def z_peer(j):
        return lax.rem(z + j, nz) * nx + x

    def x_peer(i):
        return z * nx + lax.rem(x + i, nx)

    def remote(src, dst, send, recv, seq_id, head_id):
        return pltpu.make_async_remote_copy(
            src_ref=src,
            dst_ref=dst,
            send_sem=send,
            recv_sem=recv,
            device_id=(seq_id, head_id),
            device_id_type=MESH,
        )

    barrier = pltpu.get_barrier_semaphore()
    peers = [(seq, partner)]
    peers += [(seq, y_peer(j)) for j in range(1, ny)]
    peers += [(z_peer(j), head) for j in range(1, nz)]
    peers += [(x_peer(i), head) for i in range(1, nx)]
    for peer in peers:
        pl.semaphore_signal(barrier, inc=1, device_id=peer, device_id_type=MESH)

    def weight_copy(i, j):
        source = (wk_ref, wv_ref, wq_ref)[i]
        first = pl.multiple_of(2 * width * lax.rem(y + j, ny), 2 * width)
        return pltpu.make_async_copy(
            source.at[pl.ds(first, 2 * width)], (wk, wv, wq)[i].at[j], w_sem.at[i, j]
        )

    def out_copy():
        return pltpu.make_async_copy(wo_ref, wo, o_sem)

    def block_rows(b):
        return pl.ds(pl.multiple_of(b * BLOCK_TOKENS, BLOCK_TOKENS), BLOCK_TOKENS)

    def own_copy():
        return pltpu.make_async_copy(tok_ref, xbuf.at[0, core], own_sem)

    def tok_y(b, j):
        return remote(
            tok_ref.at[block_rows(b)],
            xbuf.at[ny - j, core, block_rows(b)],
            ty_send.at[b, j - 1],
            ty_recv.at[b, j - 1],
            seq,
            y_peer(j),
        )

    def tok_core():
        return remote(tok_ref, xbuf.at[0, core], tc_send, tc_recv, seq, partner)

    def tok_core_in():
        slot = xbuf.at[0, 1 - core]
        return remote(slot, slot, tc_send, tc_recv, seq, partner)

    def tok_fwd(b, j):
        slot = xbuf.at[ny - j, core, block_rows(b)]
        return remote(slot, slot, tf_send.at[b, j - 1], tf_recv.at[b, j - 1], seq, partner)

    def tok_fwd_in(b, j):
        slot = xbuf.at[ny - j, 1 - core, block_rows(b)]
        return remote(slot, slot, tf_send.at[b, j - 1], tf_recv.at[b, j - 1], seq, partner)

    def kv_z(to):
        return remote(
            kvbuf.at[n_seq], kvbuf.at[seq], kz_send.at[to], kz_recv.at[z], to * nx + x, head
        )

    def kv_z_in(source):
        slot = kvbuf.at[source * nx + x]
        return remote(slot, slot, kz_send.at[source], kz_recv.at[source], source * nx + x, head)

    def kv_x(source, i, own):
        slot = kvbuf.at[source * nx + x]
        src = kvbuf.at[n_seq] if own else slot
        return remote(
            src, slot, kx_send.at[source, i - 1], kx_recv.at[source, i - 1], x_peer(i), head
        )

    def kv_x_in(source, i):
        slot = kvbuf.at[source * nx + lax.rem(x + nx - i, nx)]
        return remote(
            slot, slot, kx_send.at[source, i - 1], kx_recv.at[source, i - 1], x_peer(nx - i), head
        )

    def along_z(distances, act):
        for d in distances:

            @pl.when(z + d < nz)
            def _():
                act(z + d)

            @pl.when(z - d >= 0)
            def _():
                act(z - d)

    def kv_forward(distances):
        def pass_on(source):
            kv_z_in(source).wait_recv()
            for i in range(1, nx):
                kv_x(source, i, False).start()

        along_z(distances, pass_on)

    def part_core(b, j):
        return remote(
            psend.at[b, j], precv.at[b, j], p_send.at[b, j], p_recv.at[b, j], seq, partner
        )

    def part_y(b, j):
        return remote(
            ysend.at[b, j - 1],
            yrecv.at[b, j - 1],
            r_send.at[b, j - 1],
            r_recv.at[b, j - 1],
            seq,
            y_peer(j),
        )

    def send_tokens(b):
        for j in range(1, ny):
            tok_y(b, j).start()

    own_copy().start()
    for i in range(3):
        weight_copy(i, 0).start()

    lane = lax.broadcasted_iota(jnp.int32, (BLOCK_TOKENS, BLOCK_TOKENS), 1)
    row = lax.broadcasted_iota(jnp.int32, (BLOCK_TOKENS, BLOCK_TOKENS), 0)
    identity = jnp.where(lane == row, 1.0, 0.0).astype(jnp.bfloat16)
    causal = jnp.where(lane <= row, 0.0, MASKED).astype(jnp.bfloat16)

    def fill(b, carry):
        for k in range(q_cols // HEAD_SIZE):
            qbuf[b, k, :, HEAD_SIZE:] = identity
        return carry

    lax.fori_loop(0, blocks, fill, 0)
    for g in range(kv_heads):
        kcat[g, HEAD_SIZE:, DEPTH * BLOCK_TOKENS :] = causal
        vcat[g, :, HEAD_SIZE:] = jnp.ones((KEYS, HEAD_SIZE), jnp.bfloat16)

    pl.semaphore_wait(barrier, len(peers))
    send_tokens(0)
    tok_core().start()
    send_tokens(1)
    for j in range(1, ny):
        for i in range(3):
            weight_copy(i, j).start()

    def angles(b, carry):
        base = vis_ref[b, 0]
        for j in range(1, DEPTH):
            base += vis_ref[b, j]
        angle = (base + row).astype(jnp.float32) * freq_ref[...]
        cosine[b] = jnp.cos(angle)
        turn = jnp.sin(angle)
        sine[b] = jnp.where(lane < HEAD_SIZE // 2, -turn, turn)
        return carry

    lax.fori_loop(0, blocks, angles, 0)

    def scale_rows(b, j, into, into_rows):
        total = jnp.zeros((BLOCK_TOKENS, 1), jnp.float32)
        for c in range(2):
            piece = xbuf[j, c, block_rows(b)].astype(jnp.float32)
            first = (2 * lax.rem(y + j, ny) + c) * width
            gain = gain_ref[:, pl.ds(pl.multiple_of(first, width), width)]
            at = (max(j - 1, 0) * 2 + c) * width
            into[into_rows, at : at + width] = (piece * gain).astype(jnp.bfloat16)
            total += jnp.sum(piece * piece, axis=1, keepdims=True)
        return jnp.broadcast_to(total, (BLOCK_TOKENS, HEAD_SIZE))

    own_copy().wait()
    tok_core_in().wait_recv()

    def scale_own(b, carry):
        square[b] = scale_rows(b, 0, scaled, block_rows(b))
        return carry

    lax.fori_loop(0, blocks, scale_own, 0)
    for i in range(2):
        weight_copy(i, 0).wait()
    part[:, q_cols : q_cols + kv_cols] = jnp.dot(
        scaled[...], wk[0], preferred_element_type=jnp.float32
    )
    part[:, q_cols + kv_cols :] = jnp.dot(scaled[...], wv[0], preferred_element_type=jnp.float32)
    tile = 2 * HEAD_SIZE

    def own_tile(t, carry):
        cols = pl.ds(pl.multiple_of(t * tile, tile), tile)
        part[:, cols] = jnp.dot(scaled[...], wq[0, :, cols], preferred_element_type=jnp.float32)
        return carry

    def arrive(b):
        for j in range(1, ny):
            tok_y(b, j).wait_recv()
            tok_fwd(b, j).start()

        @pl.when(b < blocks - 2)
        def _():
            send_tokens(b + 2)

        @pl.when(b == 0)
        def _():
            out_copy().start()
            for j in range(1, ny):
                for i in range(2):
                    weight_copy(i, j).wait()

        rows_b = block_rows(b)

        def add_far(first, weight, cols, j):
            into = (rows_b, pl.ds(first, cols))
            part[into] += jnp.dot(far[:, (j - 1) * 2 * width : j * 2 * width], weight, preferred_element_type=jnp.float32)

        for j in range(1, ny):
            tok_fwd_in(b, j).wait_recv()
            square[b] += scale_rows(b, j, far, slice(None))
            add_far(q_cols, wk[j], kv_cols, j)
            add_far(q_cols + kv_cols, wv[j], kv_cols, j)
        scale = lax.rsqrt(square[b] / (n_head * width) + NORM_EPS)

        def rope(vectors):
            vectors = vectors * scale
            return vectors * cosine[b] + pltpu.roll(vectors, HEAD_SIZE // 2, 1) * sine[b]

        for g in range(kv_heads):
            cols = slice(g * HEAD_SIZE, (g + 1) * HEAD_SIZE)
            at = q_cols + g * HEAD_SIZE
            turned = rope(part[rows_b, at : at + HEAD_SIZE])
            kvbuf[n_seq + b, :, cols] = turned.T.astype(jnp.bfloat16)
            at += kv_cols
            cols = slice(kv_cols + g * HEAD_SIZE, kv_cols + (g + 1) * HEAD_SIZE)
            kvbuf[n_seq + b, :, cols] = (part[rows_b, at : at + HEAD_SIZE] * scale).astype(
                jnp.bfloat16
            )

        @pl.when(b == 0)
        def _():
            for i in range(1, nx):
                kv_x(z, i, True).start()
            along_z(range(1, nz), lambda to: kv_z(to).start())
            for j in range(ny):
                weight_copy(2, j).wait()
            lax.fori_loop(0, q_cols // tile, own_tile, 0)

        def query_tile(t, inner):
            first = pl.multiple_of(t * tile, tile)
            cols = pl.ds(first, tile)
            found = part[rows_b, cols]
            for j in range(1, ny):
                found += jnp.dot(
                    far[:, (j - 1) * 2 * width : j * 2 * width],
                    wq[j, :, cols],
                    preferred_element_type=jnp.float32,
                )
            for k in range(2):
                turned = rope(found[:, k * HEAD_SIZE : (k + 1) * HEAD_SIZE])
                qbuf[b, 2 * t + k, :, :HEAD_SIZE] = (turned * (HEAD_SIZE**-0.5 * LOG2E)).astype(
                    jnp.bfloat16
                )
            return inner

        lax.fori_loop(0, q_cols // tile, query_tile, 0)

        for stage, distances in enumerate(((1,), (2,), range(3, nz))):

            @pl.when(b == stage)
            def _():
                kv_forward([d for d in distances if d < nz])

    def attend(b):
        for j in range(SLOTS):
            span = slice(j * BLOCK_TOKENS, (j + 1) * BLOCK_TOKENS)
            if j < DEPTH:
                block_id = jnp.maximum(anc_ref[b, j], 0)
                owner, inside = lax.div(block_id, blocks), lax.rem(block_id, blocks)
                slot = jnp.where(owner == seq, n_seq + inside, owner)
                mask = jnp.where(lane < vis_ref[b, j], 0.0, MASKED).astype(jnp.bfloat16)
            else:
                slot = n_seq + b
            for g in range(kv_heads):
                cols = slice(g * HEAD_SIZE, (g + 1) * HEAD_SIZE)
                kcat[g, :HEAD_SIZE, span] = kvbuf[slot, :, cols]
                cols = slice(kv_cols + g * HEAD_SIZE, kv_cols + (g + 1) * HEAD_SIZE)
                vcat[g, span, :HEAD_SIZE] = kvbuf[slot, :, cols]
                if j < DEPTH:
                    kcat[g, HEAD_SIZE:, span] = mask

        for g in range(kv_heads):
            query = qbuf[b, g * group : (g + 1) * group].reshape(
                group * BLOCK_TOKENS, 2 * HEAD_SIZE
            )
            scores = jnp.dot(query, kcat[g], preferred_element_type=jnp.float32)
            top = jnp.max(scores, axis=1, keepdims=True)
            weight = jnp.exp2(scores - top).astype(jnp.bfloat16)
            mixed = jnp.dot(weight, vcat[g], preferred_element_type=jnp.float32)
            mixed = (mixed[:, :HEAD_SIZE] / mixed[:, HEAD_SIZE:]).astype(jnp.bfloat16)
            for k in range(group):
                at = (g * group + k) * HEAD_SIZE
                attn[:, at : at + HEAD_SIZE] = mixed[k * BLOCK_TOKENS : (k + 1) * BLOCK_TOKENS]

        tile = 512

        def share(j, side, store):
            base = (2 * lax.rem(y + j, ny) + side) * width

            def one_tile(t, inner):
                cols = pl.ds(pl.multiple_of(base + t * tile, tile), tile)
                into = pl.ds(pl.multiple_of(t * tile, tile), tile)
                store(into, jnp.dot(attn[...], wo[:, cols], preferred_element_type=jnp.float32))
                return inner

            lax.fori_loop(0, width // tile, one_tile, 0)

        def other_share(j):
            def store(into, found):
                psend[b, j, :, into] = found.astype(jnp.bfloat16)

            share(j, 1 - core, store)
            part_core(b, j).start()

        for j in range(1, ny):
            other_share(j)
        other_share(0)
        for j in range(1, ny):

            def put(into, found):
                far_sum[j - 1, :, into] = found

            share(j, core, put)

        def keep(into, found):
            acc[b, :, into] = found

        share(0, core, keep)
        for j in range(1, ny):
            part_core(b, j).wait_recv()
            ysend[b, j - 1] = (far_sum[j - 1] + precv[b, j].astype(jnp.float32)).astype(
                jnp.bfloat16
            )
            part_y(b, j).start()

    lag = 2

    def step(s, carry):
        @pl.when(s < blocks)
        def _():
            arrive(s)

        @pl.when(s == lag)
        def _():
            out_copy().wait()
            for source in range(nz):
                for i in range(1, nx):
                    kv_x_in(source, i).wait_recv()

        @pl.when(s >= lag)
        def _():
            attend(s - lag)

        return carry

    lax.fori_loop(0, blocks + lag, step, 0)

    def finish(b, carry):
        part_core(b, 0).wait_recv()
        result = acc[b] + precv[b, 0].astype(jnp.float32)
        for j in range(1, ny):
            part_y(b, j).wait_recv()
            result += yrecv[b, j - 1].astype(jnp.float32)
        out_ref[pl.ds(pl.multiple_of(b * BLOCK_TOKENS, BLOCK_TOKENS), BLOCK_TOKENS)] = (
            result.astype(jnp.bfloat16)
        )
        for j in range(1, ny):
            tok_y(b, j).wait_send()
            tok_fwd(b, j).wait_send()
            part_y(b, j).wait_send()
        for j in range(ny):
            part_core(b, j).wait_send()
        return carry

    lax.fori_loop(0, blocks, finish, 0)
    tok_core().wait_send()
    along_z(range(1, nz), lambda to: kv_z(to).wait_send())
    for source in range(nz):
        for i in range(1, nx):
            kv_x(source, i, True).wait_send()


def local(
    n_seq,
    n_head,
    tokens,
    norm_gain,
    w_query,
    key_weight,
    value_weight,
    w_out,
    ancestor_blocks,
    visible_counts,
):
    rows, width = tokens.shape
    blocks = rows // BLOCK_TOKENS
    q_cols = w_query.shape[1]
    kv_cols = key_weight.shape[1]
    ny = n_head // 2
    nx = ny
    nz = n_seq // nx
    half = HEAD_SIZE // 2
    frequency = ROPE_BASE ** (-(np.arange(half) * 2.0) / HEAD_SIZE)
    frequency = np.concatenate([frequency, frequency]).astype(np.float32)[None]
    dma = pltpu.SemaphoreType.DMA
    vmem = pl.BlockSpec(memory_space=pltpu.VMEM)
    smem = pl.BlockSpec(memory_space=pltpu.SMEM)
    hbm = pl.BlockSpec(memory_space=pl.ANY)
    bf16, f32 = jnp.bfloat16, jnp.float32
    return pl.pallas_call(
        functools.partial(kernel, n_seq, n_head),
        out_shape=jax.ShapeDtypeStruct((rows, width), bf16),
        in_specs=[hbm, vmem, vmem, hbm, hbm, hbm, hbm, smem, smem],
        out_specs=vmem,
        scratch_shapes=[
            pltpu.VMEM((ny, 2, rows, width), bf16),
            pltpu.VMEM((ny, 2 * width, q_cols), bf16),
            pltpu.VMEM((ny, 2 * width, kv_cols), bf16),
            pltpu.VMEM((ny, 2 * width, kv_cols), bf16),
            pltpu.VMEM(w_out.shape, bf16),
            pltpu.VMEM((rows, 2 * width), bf16),
            pltpu.VMEM((BLOCK_TOKENS, (ny - 1) * 2 * width), bf16),
            pltpu.VMEM((rows, q_cols + 2 * kv_cols), f32),
            pltpu.VMEM((blocks, BLOCK_TOKENS, HEAD_SIZE), f32),
            pltpu.VMEM((blocks, BLOCK_TOKENS, HEAD_SIZE), f32),
            pltpu.VMEM((blocks, BLOCK_TOKENS, HEAD_SIZE), f32),
            pltpu.VMEM((blocks, q_cols // HEAD_SIZE, BLOCK_TOKENS, 2 * HEAD_SIZE), bf16),
            pltpu.VMEM((n_seq + blocks, BLOCK_TOKENS, 2 * kv_cols), bf16),
            pltpu.VMEM((kv_cols // HEAD_SIZE, 2 * HEAD_SIZE, KEYS), bf16),
            pltpu.VMEM((kv_cols // HEAD_SIZE, KEYS, 2 * HEAD_SIZE), bf16),
            pltpu.VMEM((BLOCK_TOKENS, q_cols), bf16),
            pltpu.VMEM((blocks, ny, BLOCK_TOKENS, width), bf16),
            pltpu.VMEM((blocks, ny, BLOCK_TOKENS, width), bf16),
            pltpu.VMEM((ny - 1, BLOCK_TOKENS, width), f32),
            pltpu.VMEM((blocks, BLOCK_TOKENS, width), f32),
            pltpu.VMEM((blocks, ny - 1, BLOCK_TOKENS, width), bf16),
            pltpu.VMEM((blocks, ny - 1, BLOCK_TOKENS, width), bf16),
            dma((3, ny)),
            dma,
            dma,
            dma((blocks, ny - 1)),
            dma((blocks, ny - 1)),
            dma,
            dma,
            dma((blocks, ny - 1)),
            dma((blocks, ny - 1)),
            dma((nz,)),
            dma((nz,)),
            dma((nz, nx - 1)),
            dma((nz, nx - 1)),
            dma((blocks, ny)),
            dma((blocks, ny)),
            dma((blocks, ny - 1)),
            dma((blocks, ny - 1)),
        ],
        compiler_params=pltpu.CompilerParams(
            collective_id=0, has_side_effects=True, vmem_limit_bytes=60 * 1024 * 1024
        ),
        cost_estimate=pl.CostEstimate(
            flops=13 * 10**9, bytes_accessed=25 * 10**6, transcendentals=5 * 10**6
        ),
    )(
        tokens,
        norm_gain[None],
        jnp.asarray(frequency),
        w_query,
        key_weight,
        value_weight,
        w_out,
        ancestor_blocks,
        visible_counts,
    )


def solution(mesh):
    placed = (
        P("seq", "head"),
        P(),
        P(None, "head"),
        P(None, "head"),
        P(None, "head"),
        P("head", None),
        P("seq", None),
        P("seq", None),
    )
    return jax.shard_map(
        functools.partial(local, mesh.shape["seq"], mesh.shape["head"]),
        mesh=mesh,
        in_specs=placed,
        out_specs=P("seq", "head"),
        check_vma=False,
    )
```

```python
import functools

import numpy as np

import jax
import jax.numpy as jnp
from jax import lax
from jax.experimental import pallas as pl
from jax.experimental.pallas import tpu as pltpu
from jax.sharding import PartitionSpec as P

HEAD_SIZE = 128
BLOCK_TOKENS = 128
DEPTH = 8
ROPE_BASE = 500000.0
NORM_EPS = 1e-05
MESH = pl.DeviceIdType.MESH
SLOTS = DEPTH + 1
KEYS = SLOTS * BLOCK_TOKENS
LOG2E = 1.4426950408889634
MASKED = -1e30


def kernel(
    n_seq,
    n_head,
    tok_ref,
    gain_ref,
    freq_ref,
    wq_ref,
    wk_ref,
    wv_ref,
    wo_ref,
    anc_ref,
    vis_ref,
    out_ref,
    xbuf,
    wq,
    wk,
    wv,
    wo,
    scaled,
    far,
    part,
    square,
    cosine,
    sine,
    qbuf,
    kvbuf,
    kcat,
    vcat,
    attn,
    psend,
    precv,
    far_sum,
    acc,
    ysend,
    yrecv,
    w_sem,
    o_sem,
    own_sem,
    ty_send,
    ty_recv,
    tc_send,
    tc_recv,
    tf_send,
    tf_recv,
    kz_send,
    kz_recv,
    kx_send,
    kx_recv,
    p_send,
    p_recv,
    r_send,
    r_recv,
):
    rows, width = tok_ref.shape
    blocks = rows // BLOCK_TOKENS
    q_cols = wq.shape[2]
    kv_cols = wk.shape[2]
    kv_heads = kv_cols // HEAD_SIZE
    group = q_cols // kv_cols
    ny = n_head // 2
    nx = ny
    nz = n_seq // nx
    seq = lax.axis_index("seq")
    head = lax.axis_index("head")
    y, core = lax.div(head, 2), lax.rem(head, 2)
    z, x = lax.div(seq, nx), lax.rem(seq, nx)
    partner = 2 * y + 1 - core

    def y_peer(j):
        return 2 * lax.rem(y + j, ny) + core

    def z_peer(j):
        return lax.rem(z + j, nz) * nx + x

    def x_peer(i):
        return z * nx + lax.rem(x + i, nx)

    def remote(src, dst, send, recv, seq_id, head_id):
        return pltpu.make_async_remote_copy(
            src_ref=src,
            dst_ref=dst,
            send_sem=send,
            recv_sem=recv,
            device_id=(seq_id, head_id),
            device_id_type=MESH,
        )

    barrier = pltpu.get_barrier_semaphore()
    peers = [(seq, partner)]
    peers += [(seq, y_peer(j)) for j in range(1, ny)]
    peers += [(z_peer(j), head) for j in range(1, nz)]
    peers += [(x_peer(i), head) for i in range(1, nx)]
    for peer in peers:
        pl.semaphore_signal(barrier, inc=1, device_id=peer, device_id_type=MESH)

    def weight_copy(i, j):
        source = (wk_ref, wv_ref, wq_ref)[i]
        first = pl.multiple_of(2 * width * lax.rem(y + j, ny), 2 * width)
        return pltpu.make_async_copy(
            source.at[pl.ds(first, 2 * width)], (wk, wv, wq)[i].at[j], w_sem.at[i, j]
        )

    def out_copy():
        return pltpu.make_async_copy(wo_ref, wo, o_sem)

    def block_rows(b):
        return pl.ds(pl.multiple_of(b * BLOCK_TOKENS, BLOCK_TOKENS), BLOCK_TOKENS)

    def own_copy():
        return pltpu.make_async_copy(tok_ref, xbuf.at[0, core], own_sem)

    def tok_y(b, j):
        return remote(
            tok_ref.at[block_rows(b)],
            xbuf.at[ny - j, core, block_rows(b)],
            ty_send.at[b, j - 1],
            ty_recv.at[b, j - 1],
            seq,
            y_peer(j),
        )

    def tok_core():
        return remote(tok_ref, xbuf.at[0, core], tc_send, tc_recv, seq, partner)

    def tok_core_in():
        slot = xbuf.at[0, 1 - core]
        return remote(slot, slot, tc_send, tc_recv, seq, partner)

    def tok_fwd(b, j):
        slot = xbuf.at[ny - j, core, block_rows(b)]
        return remote(slot, slot, tf_send.at[b, j - 1], tf_recv.at[b, j - 1], seq, partner)

    def tok_fwd_in(b, j):
        slot = xbuf.at[ny - j, 1 - core, block_rows(b)]
        return remote(slot, slot, tf_send.at[b, j - 1], tf_recv.at[b, j - 1], seq, partner)

    def kv_own(way):
        return remote(
            kvbuf.at[n_seq],
            kvbuf.at[seq],
            kz_send.at[nz + (way + 1) // 2],
            kz_recv.at[z],
            (z + way) * nx + x,
            head,
        )

    def kv_hop(source, way):
        slot = kvbuf.at[source * nx + x]
        return remote(
            slot, slot, kz_send.at[source], kz_recv.at[source], (z + way) * nx + x, head
        )

    def kv_x(source, i, own):
        slot = kvbuf.at[source * nx + x]
        src = kvbuf.at[n_seq] if own else slot
        return remote(
            src, slot, kx_send.at[source, i - 1], kx_recv.at[source, i - 1], x_peer(i), head
        )

    def kv_x_in(source, i):
        slot = kvbuf.at[source * nx + lax.rem(x + nx - i, nx)]
        return remote(
            slot, slot, kx_send.at[source, i - 1], kx_recv.at[source, i - 1], x_peer(nx - i), head
        )

    def own_z(act):
        for way in (1, -1):

            @pl.when((z + way >= 0) & (z + way < nz))
            def _():
                act(kv_own(way))

    def along_z(distances, arrived, onward):
        for d in distances:
            for way in (1, -1):
                source = z - way * d

                @pl.when((source >= 0) & (source < nz))
                def _():
                    arrived(source, way)

                    @pl.when((z + way >= 0) & (z + way < nz))
                    def _():
                        onward(kv_hop(source, way))

    def kv_forward(distances):
        def arrived(source, way):
            kv_hop(source, -way).wait_recv()
            for i in range(1, nx):
                kv_x(source, i, False).start()

        along_z(distances, arrived, lambda copy: copy.start())

    def part_core(b, j):
        return remote(
            psend.at[b, j], precv.at[b, j], p_send.at[b, j], p_recv.at[b, j], seq, partner
        )

    def part_y(b, j):
        return remote(
            ysend.at[b, j - 1],
            yrecv.at[b, j - 1],
            r_send.at[b, j - 1],
            r_recv.at[b, j - 1],
            seq,
            y_peer(j),
        )

    def send_tokens(b):
        for j in range(1, ny):
            tok_y(b, j).start()

    own_copy().start()
    for i in range(3):
        weight_copy(i, 0).start()

    lane = lax.broadcasted_iota(jnp.int32, (BLOCK_TOKENS, BLOCK_TOKENS), 1)
    row = lax.broadcasted_iota(jnp.int32, (BLOCK_TOKENS, BLOCK_TOKENS), 0)
    identity = jnp.where(lane == row, 1.0, 0.0).astype(jnp.bfloat16)
    causal = jnp.where(lane <= row, 0.0, MASKED).astype(jnp.bfloat16)

    def fill(b, carry):
        for k in range(q_cols // HEAD_SIZE):
            qbuf[b, k, :, HEAD_SIZE:] = identity
        return carry

    lax.fori_loop(0, blocks, fill, 0)
    for g in range(kv_heads):
        kcat[g, HEAD_SIZE:, DEPTH * BLOCK_TOKENS :] = causal
        vcat[g, :, HEAD_SIZE:] = jnp.ones((KEYS, HEAD_SIZE), jnp.bfloat16)

    pl.semaphore_wait(barrier, len(peers))
    send_tokens(0)
    tok_core().start()
    send_tokens(1)
    for j in range(1, ny):
        for i in range(3):
            weight_copy(i, j).start()

    def angles(b, carry):
        base = vis_ref[b, 0]
        for j in range(1, DEPTH):
            base += vis_ref[b, j]
        angle = (base + row).astype(jnp.float32) * freq_ref[...]
        cosine[b] = jnp.cos(angle)
        turn = jnp.sin(angle)
        sine[b] = jnp.where(lane < HEAD_SIZE // 2, -turn, turn)
        return carry

    lax.fori_loop(0, blocks, angles, 0)

    def scale_rows(b, j, into, into_rows):
        total = jnp.zeros((BLOCK_TOKENS, 1), jnp.float32)
        for c in range(2):
            piece = xbuf[j, c, block_rows(b)].astype(jnp.float32)
            first = (2 * lax.rem(y + j, ny) + c) * width
            gain = gain_ref[:, pl.ds(pl.multiple_of(first, width), width)]
            at = (max(j - 1, 0) * 2 + c) * width
            into[into_rows, at : at + width] = (piece * gain).astype(jnp.bfloat16)
            total += jnp.sum(piece * piece, axis=1, keepdims=True)
        return jnp.broadcast_to(total, (BLOCK_TOKENS, HEAD_SIZE))

    own_copy().wait()
    tok_core_in().wait_recv()

    def scale_own(b, carry):
        square[b] = scale_rows(b, 0, scaled, block_rows(b))
        return carry

    lax.fori_loop(0, blocks, scale_own, 0)
    for i in range(2):
        weight_copy(i, 0).wait()
    part[:, q_cols : q_cols + kv_cols] = jnp.dot(
        scaled[...], wk[0], preferred_element_type=jnp.float32
    )
    part[:, q_cols + kv_cols :] = jnp.dot(scaled[...], wv[0], preferred_element_type=jnp.float32)
    tile = 2 * HEAD_SIZE

    def own_tile(t, carry):
        cols = pl.ds(pl.multiple_of(t * tile, tile), tile)
        part[:, cols] = jnp.dot(scaled[...], wq[0, :, cols], preferred_element_type=jnp.float32)
        return carry

    def arrive(b):
        for j in range(1, ny):
            tok_y(b, j).wait_recv()
            tok_fwd(b, j).start()

        @pl.when(b < blocks - 2)
        def _():
            send_tokens(b + 2)

        @pl.when(b == 0)
        def _():
            out_copy().start()
            for j in range(1, ny):
                for i in range(2):
                    weight_copy(i, j).wait()

        rows_b = block_rows(b)

        def add_far(first, weight, cols, j):
            into = (rows_b, pl.ds(first, cols))
            part[into] += jnp.dot(far[:, (j - 1) * 2 * width : j * 2 * width], weight, preferred_element_type=jnp.float32)

        for j in range(1, ny):
            tok_fwd_in(b, j).wait_recv()
            square[b] += scale_rows(b, j, far, slice(None))
            add_far(q_cols, wk[j], kv_cols, j)
            add_far(q_cols + kv_cols, wv[j], kv_cols, j)
        scale = lax.rsqrt(square[b] / (n_head * width) + NORM_EPS)

        def rope(vectors):
            vectors = vectors * scale
            return vectors * cosine[b] + pltpu.roll(vectors, HEAD_SIZE // 2, 1) * sine[b]

        for g in range(kv_heads):
            cols = slice(g * HEAD_SIZE, (g + 1) * HEAD_SIZE)
            at = q_cols + g * HEAD_SIZE
            turned = rope(part[rows_b, at : at + HEAD_SIZE])
            kvbuf[n_seq + b, :, cols] = turned.T.astype(jnp.bfloat16)
            at += kv_cols
            cols = slice(kv_cols + g * HEAD_SIZE, kv_cols + (g + 1) * HEAD_SIZE)
            kvbuf[n_seq + b, :, cols] = (part[rows_b, at : at + HEAD_SIZE] * scale).astype(
                jnp.bfloat16
            )

        @pl.when(b == 0)
        def _():
            for i in range(1, nx):
                kv_x(z, i, True).start()
            own_z(lambda copy: copy.start())
            for j in range(ny):
                weight_copy(2, j).wait()
            lax.fori_loop(0, q_cols // tile, own_tile, 0)

        def query_tile(t, inner):
            first = pl.multiple_of(t * tile, tile)
            cols = pl.ds(first, tile)
            found = part[rows_b, cols]
            for j in range(1, ny):
                found += jnp.dot(
                    far[:, (j - 1) * 2 * width : j * 2 * width],
                    wq[j, :, cols],
                    preferred_element_type=jnp.float32,
                )
            for k in range(2):
                turned = rope(found[:, k * HEAD_SIZE : (k + 1) * HEAD_SIZE])
                qbuf[b, 2 * t + k, :, :HEAD_SIZE] = (turned * (HEAD_SIZE**-0.5 * LOG2E)).astype(
                    jnp.bfloat16
                )
            return inner

        lax.fori_loop(0, q_cols // tile, query_tile, 0)

        for stage, distances in enumerate(((1,), (2,), range(3, nz))):

            @pl.when(b == stage)
            def _():
                kv_forward([d for d in distances if d < nz])

    def attend(b):
        for j in range(SLOTS):
            span = slice(j * BLOCK_TOKENS, (j + 1) * BLOCK_TOKENS)
            if j < DEPTH:
                block_id = jnp.maximum(anc_ref[b, j], 0)
                owner, inside = lax.div(block_id, blocks), lax.rem(block_id, blocks)
                slot = jnp.where(owner == seq, n_seq + inside, owner)
                mask = jnp.where(lane < vis_ref[b, j], 0.0, MASKED).astype(jnp.bfloat16)
            else:
                slot = n_seq + b
            for g in range(kv_heads):
                cols = slice(g * HEAD_SIZE, (g + 1) * HEAD_SIZE)
                kcat[g, :HEAD_SIZE, span] = kvbuf[slot, :, cols]
                cols = slice(kv_cols + g * HEAD_SIZE, kv_cols + (g + 1) * HEAD_SIZE)
                vcat[g, span, :HEAD_SIZE] = kvbuf[slot, :, cols]
                if j < DEPTH:
                    kcat[g, HEAD_SIZE:, span] = mask

        for g in range(kv_heads):
            query = qbuf[b, g * group : (g + 1) * group].reshape(
                group * BLOCK_TOKENS, 2 * HEAD_SIZE
            )
            scores = jnp.dot(query, kcat[g], preferred_element_type=jnp.float32)
            top = jnp.max(scores, axis=1, keepdims=True)
            weight = jnp.exp2(scores - top).astype(jnp.bfloat16)
            mixed = jnp.dot(weight, vcat[g], preferred_element_type=jnp.float32)
            mixed = (mixed[:, :HEAD_SIZE] / mixed[:, HEAD_SIZE:]).astype(jnp.bfloat16)
            for k in range(group):
                at = (g * group + k) * HEAD_SIZE
                attn[:, at : at + HEAD_SIZE] = mixed[k * BLOCK_TOKENS : (k + 1) * BLOCK_TOKENS]

        tile = 512

        def share(j, side, store):
            base = (2 * lax.rem(y + j, ny) + side) * width

            def one_tile(t, inner):
                cols = pl.ds(pl.multiple_of(base + t * tile, tile), tile)
                into = pl.ds(pl.multiple_of(t * tile, tile), tile)
                store(into, jnp.dot(attn[...], wo[:, cols], preferred_element_type=jnp.float32))
                return inner

            lax.fori_loop(0, width // tile, one_tile, 0)

        def other_share(j):
            def store(into, found):
                psend[b, j, :, into] = found.astype(jnp.bfloat16)

            share(j, 1 - core, store)
            part_core(b, j).start()

        for j in range(1, ny):
            other_share(j)
        other_share(0)
        for j in range(1, ny):

            def put(into, found):
                far_sum[j - 1, :, into] = found

            share(j, core, put)

        def keep(into, found):
            acc[b, :, into] = found

        share(0, core, keep)
        for j in range(1, ny):
            part_core(b, j).wait_recv()
            ysend[b, j - 1] = (far_sum[j - 1] + precv[b, j].astype(jnp.float32)).astype(
                jnp.bfloat16
            )
            part_y(b, j).start()

    lag = 2

    def step(s, carry):
        @pl.when(s < blocks)
        def _():
            arrive(s)

        @pl.when(s == lag)
        def _():
            out_copy().wait()
            for source in range(nz):
                for i in range(1, nx):
                    kv_x_in(source, i).wait_recv()

        @pl.when(s >= lag)
        def _():
            attend(s - lag)

        return carry

    lax.fori_loop(0, blocks + lag, step, 0)

    def finish(b, carry):
        part_core(b, 0).wait_recv()
        result = acc[b] + precv[b, 0].astype(jnp.float32)
        for j in range(1, ny):
            part_y(b, j).wait_recv()
            result += yrecv[b, j - 1].astype(jnp.float32)
        out_ref[pl.ds(pl.multiple_of(b * BLOCK_TOKENS, BLOCK_TOKENS), BLOCK_TOKENS)] = (
            result.astype(jnp.bfloat16)
        )
        for j in range(1, ny):
            tok_y(b, j).wait_send()
            tok_fwd(b, j).wait_send()
            part_y(b, j).wait_send()
        for j in range(ny):
            part_core(b, j).wait_send()
        return carry

    lax.fori_loop(0, blocks, finish, 0)
    tok_core().wait_send()
    own_z(lambda copy: copy.wait_send())
    along_z(range(1, nz), lambda source, way: None, lambda copy: copy.wait_send())
    for source in range(nz):
        for i in range(1, nx):
            kv_x(source, i, True).wait_send()


def local(
    n_seq,
    n_head,
    tokens,
    norm_gain,
    w_query,
    key_weight,
    value_weight,
    w_out,
    ancestor_blocks,
    visible_counts,
):
    rows, width = tokens.shape
    blocks = rows // BLOCK_TOKENS
    q_cols = w_query.shape[1]
    kv_cols = key_weight.shape[1]
    ny = n_head // 2
    nx = ny
    nz = n_seq // nx
    half = HEAD_SIZE // 2
    frequency = ROPE_BASE ** (-(np.arange(half) * 2.0) / HEAD_SIZE)
    frequency = np.concatenate([frequency, frequency]).astype(np.float32)[None]
    dma = pltpu.SemaphoreType.DMA
    vmem = pl.BlockSpec(memory_space=pltpu.VMEM)
    smem = pl.BlockSpec(memory_space=pltpu.SMEM)
    hbm = pl.BlockSpec(memory_space=pl.ANY)
    bf16, f32 = jnp.bfloat16, jnp.float32
    return pl.pallas_call(
        functools.partial(kernel, n_seq, n_head),
        out_shape=jax.ShapeDtypeStruct((rows, width), bf16),
        in_specs=[hbm, vmem, vmem, hbm, hbm, hbm, hbm, smem, smem],
        out_specs=vmem,
        scratch_shapes=[
            pltpu.VMEM((ny, 2, rows, width), bf16),
            pltpu.VMEM((ny, 2 * width, q_cols), bf16),
            pltpu.VMEM((ny, 2 * width, kv_cols), bf16),
            pltpu.VMEM((ny, 2 * width, kv_cols), bf16),
            pltpu.VMEM(w_out.shape, bf16),
            pltpu.VMEM((rows, 2 * width), bf16),
            pltpu.VMEM((BLOCK_TOKENS, (ny - 1) * 2 * width), bf16),
            pltpu.VMEM((rows, q_cols + 2 * kv_cols), f32),
            pltpu.VMEM((blocks, BLOCK_TOKENS, HEAD_SIZE), f32),
            pltpu.VMEM((blocks, BLOCK_TOKENS, HEAD_SIZE), f32),
            pltpu.VMEM((blocks, BLOCK_TOKENS, HEAD_SIZE), f32),
            pltpu.VMEM((blocks, q_cols // HEAD_SIZE, BLOCK_TOKENS, 2 * HEAD_SIZE), bf16),
            pltpu.VMEM((n_seq + blocks, BLOCK_TOKENS, 2 * kv_cols), bf16),
            pltpu.VMEM((kv_cols // HEAD_SIZE, 2 * HEAD_SIZE, KEYS), bf16),
            pltpu.VMEM((kv_cols // HEAD_SIZE, KEYS, 2 * HEAD_SIZE), bf16),
            pltpu.VMEM((BLOCK_TOKENS, q_cols), bf16),
            pltpu.VMEM((blocks, ny, BLOCK_TOKENS, width), bf16),
            pltpu.VMEM((blocks, ny, BLOCK_TOKENS, width), bf16),
            pltpu.VMEM((ny - 1, BLOCK_TOKENS, width), f32),
            pltpu.VMEM((blocks, BLOCK_TOKENS, width), f32),
            pltpu.VMEM((blocks, ny - 1, BLOCK_TOKENS, width), bf16),
            pltpu.VMEM((blocks, ny - 1, BLOCK_TOKENS, width), bf16),
            dma((3, ny)),
            dma,
            dma,
            dma((blocks, ny - 1)),
            dma((blocks, ny - 1)),
            dma,
            dma,
            dma((blocks, ny - 1)),
            dma((blocks, ny - 1)),
            dma((nz + 2,)),
            dma((nz,)),
            dma((nz, nx - 1)),
            dma((nz, nx - 1)),
            dma((blocks, ny)),
            dma((blocks, ny)),
            dma((blocks, ny - 1)),
            dma((blocks, ny - 1)),
        ],
        compiler_params=pltpu.CompilerParams(
            collective_id=0, has_side_effects=True, vmem_limit_bytes=60 * 1024 * 1024
        ),
        cost_estimate=pl.CostEstimate(
            flops=13 * 10**9, bytes_accessed=25 * 10**6, transcendentals=5 * 10**6
        ),
    )(
        tokens,
        norm_gain[None],
        jnp.asarray(frequency),
        w_query,
        key_weight,
        value_weight,
        w_out,
        ancestor_blocks,
        visible_counts,
    )


def solution(mesh):
    placed = (
        P("seq", "head"),
        P(),
        P(None, "head"),
        P(None, "head"),
        P(None, "head"),
        P("head", None),
        P("seq", None),
        P("seq", None),
    )
    return jax.shard_map(
        functools.partial(local, mesh.shape["seq"], mesh.shape["head"]),
        mesh=mesh,
        in_specs=placed,
        out_specs=P("seq", "head"),
        check_vma=False,
    )
```

```python
import functools

import numpy as np

import jax
import jax.numpy as jnp
from jax import lax
from jax.experimental import pallas as pl
from jax.experimental.pallas import tpu as pltpu
from jax.sharding import PartitionSpec as P

HEAD_SIZE = 128
BLOCK_TOKENS = 128
DEPTH = 8
ROPE_BASE = 500000.0
NORM_EPS = 1e-05
MESH = pl.DeviceIdType.MESH
SLOTS = DEPTH + 1
KEYS = SLOTS * BLOCK_TOKENS
LOG2E = 1.4426950408889634
MASKED = -1e30


def kernel(
    n_seq,
    n_head,
    tok_ref,
    gain_ref,
    freq_ref,
    wq_ref,
    wk_ref,
    wv_ref,
    wo_ref,
    anc_ref,
    vis_ref,
    out_ref,
    xbuf,
    wq,
    wk,
    wv,
    wo,
    scaled,
    far,
    part,
    square,
    cosine,
    sine,
    qbuf,
    kvbuf,
    kcat,
    vcat,
    attn,
    psend,
    precv,
    far_sum,
    acc,
    ysend,
    yrecv,
    w_sem,
    o_sem,
    own_sem,
    ty_send,
    ty_recv,
    tc_send,
    tc_recv,
    tf_send,
    tf_recv,
    kz_send,
    kz_recv,
    kx_send,
    kx_recv,
    p_send,
    p_recv,
    r_send,
    r_recv,
):
    rows, width = tok_ref.shape
    blocks = rows // BLOCK_TOKENS
    q_cols = wq.shape[2]
    kv_cols = wk.shape[2]
    kv_heads = kv_cols // HEAD_SIZE
    group = q_cols // kv_cols
    ny = n_head // 2
    nx = ny
    nz = n_seq // nx
    seq = lax.axis_index("seq")
    head = lax.axis_index("head")
    y, core = lax.div(head, 2), lax.rem(head, 2)
    z, x = lax.div(seq, nx), lax.rem(seq, nx)
    partner = 2 * y + 1 - core

    def y_peer(j):
        return 2 * lax.rem(y + j, ny) + core

    def z_peer(j):
        return lax.rem(z + j, nz) * nx + x

    def x_peer(i):
        return z * nx + lax.rem(x + i, nx)

    def remote(src, dst, send, recv, seq_id, head_id):
        return pltpu.make_async_remote_copy(
            src_ref=src,
            dst_ref=dst,
            send_sem=send,
            recv_sem=recv,
            device_id=(seq_id, head_id),
            device_id_type=MESH,
        )

    barrier = pltpu.get_barrier_semaphore()
    peers = [(seq, partner)]
    peers += [(seq, y_peer(j)) for j in range(1, ny)]
    peers += [(z_peer(j), head) for j in range(1, nz)]
    peers += [(x_peer(i), head) for i in range(1, nx)]
    for peer in peers:
        pl.semaphore_signal(barrier, inc=1, device_id=peer, device_id_type=MESH)

    def weight_copy(i, j):
        source = (wk_ref, wv_ref, wq_ref)[i]
        first = pl.multiple_of(2 * width * lax.rem(y + j, ny), 2 * width)
        return pltpu.make_async_copy(
            source.at[pl.ds(first, 2 * width)], (wk, wv, wq)[i].at[j], w_sem.at[i, j]
        )

    def out_copy():
        return pltpu.make_async_copy(wo_ref, wo, o_sem)

    def block_rows(b):
        return pl.ds(pl.multiple_of(b * BLOCK_TOKENS, BLOCK_TOKENS), BLOCK_TOKENS)

    def own_copy():
        return pltpu.make_async_copy(tok_ref, xbuf.at[0, core], own_sem)

    def tok_y(b, j):
        return remote(
            tok_ref.at[block_rows(b)],
            xbuf.at[ny - j, core, block_rows(b)],
            ty_send.at[b, j - 1],
            ty_recv.at[b, j - 1],
            seq,
            y_peer(j),
        )

    def tok_core():
        return remote(tok_ref, xbuf.at[0, core], tc_send, tc_recv, seq, partner)

    def tok_core_in():
        slot = xbuf.at[0, 1 - core]
        return remote(slot, slot, tc_send, tc_recv, seq, partner)

    def tok_fwd(b, j):
        slot = xbuf.at[ny - j, core, block_rows(b)]
        return remote(slot, slot, tf_send.at[b, j - 1], tf_recv.at[b, j - 1], seq, partner)

    def tok_fwd_in(b, j):
        slot = xbuf.at[ny - j, 1 - core, block_rows(b)]
        return remote(slot, slot, tf_send.at[b, j - 1], tf_recv.at[b, j - 1], seq, partner)

    def kv_own(way):
        return remote(
            kvbuf.at[n_seq],
            kvbuf.at[seq],
            kz_send.at[nz + (way + 1) // 2],
            kz_recv.at[z],
            (z + way) * nx + x,
            head,
        )

    def kv_hop(source, way):
        slot = kvbuf.at[source * nx + x]
        return remote(
            slot, slot, kz_send.at[source], kz_recv.at[source], (z + way) * nx + x, head
        )

    def kv_x(source, i, own):
        slot = kvbuf.at[source * nx + x]
        src = kvbuf.at[n_seq] if own else slot
        return remote(
            src, slot, kx_send.at[source, i - 1], kx_recv.at[source, i - 1], x_peer(i), head
        )

    def kv_x_in(source, i):
        slot = kvbuf.at[source * nx + lax.rem(x + nx - i, nx)]
        return remote(
            slot, slot, kx_send.at[source, i - 1], kx_recv.at[source, i - 1], x_peer(nx - i), head
        )

    def own_z(act):
        for way in (1, -1):

            @pl.when((z + way >= 0) & (z + way < nz))
            def _():
                act(kv_own(way))

    def along_z(distances, arrived, onward):
        for d in distances:
            for way in (1, -1):
                source = z - way * d

                @pl.when((source >= 0) & (source < nz))
                def _():
                    arrived(source, way)

                    @pl.when((z + way >= 0) & (z + way < nz))
                    def _():
                        onward(kv_hop(source, way))

    def kv_forward(distances):
        def arrived(source, way):
            kv_hop(source, -way).wait_recv()
            for i in range(1, nx):
                kv_x(source, i, False).start()

        along_z(distances, arrived, lambda copy: copy.start())

    def part_core(b, j):
        return remote(
            psend.at[b, j], precv.at[b, j], p_send.at[b, j], p_recv.at[b, j], seq, partner
        )

    def part_y(b, j):
        return remote(
            ysend.at[b, j - 1],
            yrecv.at[b, j - 1],
            r_send.at[b, j - 1],
            r_recv.at[b, j - 1],
            seq,
            y_peer(j),
        )

    def send_tokens(b):
        for j in range(1, ny):
            tok_y(b, j).start()

    own_copy().start()
    for i in range(3):
        weight_copy(i, 0).start()

    lane = lax.broadcasted_iota(jnp.int32, (BLOCK_TOKENS, BLOCK_TOKENS), 1)
    row = lax.broadcasted_iota(jnp.int32, (BLOCK_TOKENS, BLOCK_TOKENS), 0)
    identity = jnp.where(lane == row, 1.0, 0.0).astype(jnp.bfloat16)
    causal = jnp.where(lane <= row, 0.0, MASKED).astype(jnp.bfloat16)

    def fill(b, carry):
        for k in range(q_cols // HEAD_SIZE):
            qbuf[b, k, :, HEAD_SIZE:] = identity
        return carry

    lax.fori_loop(0, blocks, fill, 0)
    for g in range(kv_heads):
        kcat[g, HEAD_SIZE:, DEPTH * BLOCK_TOKENS :] = causal
        vcat[g, :, HEAD_SIZE:] = jnp.ones((KEYS, HEAD_SIZE), jnp.bfloat16)

    pl.semaphore_wait(barrier, len(peers))
    send_tokens(0)
    tok_core().start()
    for b in range(1, blocks):
        send_tokens(b)
    for j in range(1, ny):
        for i in range(3):
            weight_copy(i, j).start()

    def angles(b, carry):
        base = vis_ref[b, 0]
        for j in range(1, DEPTH):
            base += vis_ref[b, j]
        angle = (base + row).astype(jnp.float32) * freq_ref[...]
        cosine[b] = jnp.cos(angle)
        turn = jnp.sin(angle)
        sine[b] = jnp.where(lane < HEAD_SIZE // 2, -turn, turn)
        return carry

    lax.fori_loop(0, blocks, angles, 0)

    def scale_rows(b, j, into, into_rows):
        total = jnp.zeros((BLOCK_TOKENS, 1), jnp.float32)
        for c in range(2):
            piece = xbuf[j, c, block_rows(b)].astype(jnp.float32)
            first = (2 * lax.rem(y + j, ny) + c) * width
            gain = gain_ref[:, pl.ds(pl.multiple_of(first, width), width)]
            at = (max(j - 1, 0) * 2 + c) * width
            into[into_rows, at : at + width] = (piece * gain).astype(jnp.bfloat16)
            total += jnp.sum(piece * piece, axis=1, keepdims=True)
        return jnp.broadcast_to(total, (BLOCK_TOKENS, HEAD_SIZE))

    own_copy().wait()
    tok_core_in().wait_recv()

    def scale_own(b, carry):
        square[b] = scale_rows(b, 0, scaled, block_rows(b))
        return carry

    lax.fori_loop(0, blocks, scale_own, 0)
    for i in range(2):
        weight_copy(i, 0).wait()
    part[:, q_cols : q_cols + kv_cols] = jnp.dot(
        scaled[...], wk[0], preferred_element_type=jnp.float32
    )
    part[:, q_cols + kv_cols :] = jnp.dot(scaled[...], wv[0], preferred_element_type=jnp.float32)
    tile = 2 * HEAD_SIZE

    def own_tile(t, carry):
        cols = pl.ds(pl.multiple_of(t * tile, tile), tile)
        part[:, cols] = jnp.dot(scaled[...], wq[0, :, cols], preferred_element_type=jnp.float32)
        return carry

    def arrive(b):
        for j in range(1, ny):
            tok_y(b, j).wait_recv()
            tok_fwd(b, j).start()

        @pl.when(b == 0)
        def _():
            out_copy().start()
            for j in range(1, ny):
                for i in range(2):
                    weight_copy(i, j).wait()

        rows_b = block_rows(b)

        def add_far(first, weight, cols, j):
            into = (rows_b, pl.ds(first, cols))
            part[into] += jnp.dot(far[:, (j - 1) * 2 * width : j * 2 * width], weight, preferred_element_type=jnp.float32)

        for j in range(1, ny):
            tok_fwd_in(b, j).wait_recv()
            square[b] += scale_rows(b, j, far, slice(None))
            add_far(q_cols, wk[j], kv_cols, j)
            add_far(q_cols + kv_cols, wv[j], kv_cols, j)
        scale = lax.rsqrt(square[b] / (n_head * width) + NORM_EPS)

        def rope(vectors):
            vectors = vectors * scale
            return vectors * cosine[b] + pltpu.roll(vectors, HEAD_SIZE // 2, 1) * sine[b]

        for g in range(kv_heads):
            cols = slice(g * HEAD_SIZE, (g + 1) * HEAD_SIZE)
            at = q_cols + g * HEAD_SIZE
            turned = rope(part[rows_b, at : at + HEAD_SIZE])
            kvbuf[n_seq + b, :, cols] = turned.T.astype(jnp.bfloat16)
            at += kv_cols
            cols = slice(kv_cols + g * HEAD_SIZE, kv_cols + (g + 1) * HEAD_SIZE)
            kvbuf[n_seq + b, :, cols] = (part[rows_b, at : at + HEAD_SIZE] * scale).astype(
                jnp.bfloat16
            )

        @pl.when(b == 0)
        def _():
            for i in range(1, nx):
                kv_x(z, i, True).start()
            own_z(lambda copy: copy.start())
            for j in range(ny):
                weight_copy(2, j).wait()
            lax.fori_loop(0, q_cols // tile, own_tile, 0)

        def query_tile(t, inner):
            first = pl.multiple_of(t * tile, tile)
            cols = pl.ds(first, tile)
            found = part[rows_b, cols]
            for j in range(1, ny):
                found += jnp.dot(
                    far[:, (j - 1) * 2 * width : j * 2 * width],
                    wq[j, :, cols],
                    preferred_element_type=jnp.float32,
                )
            for k in range(2):
                turned = rope(found[:, k * HEAD_SIZE : (k + 1) * HEAD_SIZE])
                qbuf[b, 2 * t + k, :, :HEAD_SIZE] = (turned * (HEAD_SIZE**-0.5 * LOG2E)).astype(
                    jnp.bfloat16
                )
            return inner

        lax.fori_loop(0, q_cols // tile, query_tile, 0)

        for stage, distances in enumerate(((1,), (2,), range(3, nz))):

            @pl.when(b == stage)
            def _():
                kv_forward([d for d in distances if d < nz])

    def attend(b):
        for j in range(SLOTS):
            span = slice(j * BLOCK_TOKENS, (j + 1) * BLOCK_TOKENS)
            if j < DEPTH:
                block_id = jnp.maximum(anc_ref[b, j], 0)
                owner, inside = lax.div(block_id, blocks), lax.rem(block_id, blocks)
                slot = jnp.where(owner == seq, n_seq + inside, owner)
                mask = jnp.where(lane < vis_ref[b, j], 0.0, MASKED).astype(jnp.bfloat16)
            else:
                slot = n_seq + b
            for g in range(kv_heads):
                cols = slice(g * HEAD_SIZE, (g + 1) * HEAD_SIZE)
                kcat[g, :HEAD_SIZE, span] = kvbuf[slot, :, cols]
                cols = slice(kv_cols + g * HEAD_SIZE, kv_cols + (g + 1) * HEAD_SIZE)
                vcat[g, span, :HEAD_SIZE] = kvbuf[slot, :, cols]
                if j < DEPTH:
                    kcat[g, HEAD_SIZE:, span] = mask

        for g in range(kv_heads):
            query = qbuf[b, g * group : (g + 1) * group].reshape(
                group * BLOCK_TOKENS, 2 * HEAD_SIZE
            )
            scores = jnp.dot(query, kcat[g], preferred_element_type=jnp.float32)
            top = jnp.max(scores, axis=1, keepdims=True)
            weight = jnp.exp2(scores - top).astype(jnp.bfloat16)
            mixed = jnp.dot(weight, vcat[g], preferred_element_type=jnp.float32)
            mixed = (mixed[:, :HEAD_SIZE] / mixed[:, HEAD_SIZE:]).astype(jnp.bfloat16)
            for k in range(group):
                at = (g * group + k) * HEAD_SIZE
                attn[:, at : at + HEAD_SIZE] = mixed[k * BLOCK_TOKENS : (k + 1) * BLOCK_TOKENS]

        tile = 512

        def share(j, side, store):
            base = (2 * lax.rem(y + j, ny) + side) * width

            def one_tile(t, inner):
                cols = pl.ds(pl.multiple_of(base + t * tile, tile), tile)
                into = pl.ds(pl.multiple_of(t * tile, tile), tile)
                store(into, jnp.dot(attn[...], wo[:, cols], preferred_element_type=jnp.float32))
                return inner

            lax.fori_loop(0, width // tile, one_tile, 0)

        def other_share(j):
            def store(into, found):
                psend[b, j, :, into] = found.astype(jnp.bfloat16)

            share(j, 1 - core, store)
            part_core(b, j).start()

        for j in range(1, ny):
            other_share(j)
        other_share(0)
        for j in range(1, ny):

            def put(into, found):
                far_sum[j - 1, :, into] = found

            share(j, core, put)

        def keep(into, found):
            acc[b, :, into] = found

        share(0, core, keep)
        for j in range(1, ny):
            part_core(b, j).wait_recv()
            ysend[b, j - 1] = (far_sum[j - 1] + precv[b, j].astype(jnp.float32)).astype(
                jnp.bfloat16
            )
            part_y(b, j).start()

    lag = 3

    def step(s, carry):
        @pl.when(s < blocks)
        def _():
            arrive(s)

        @pl.when(s == lag)
        def _():
            out_copy().wait()
            for source in range(nz):
                for i in range(1, nx):
                    kv_x_in(source, i).wait_recv()

        @pl.when(s >= lag)
        def _():
            attend(s - lag)

        return carry

    lax.fori_loop(0, blocks + lag, step, 0)

    def finish(b, carry):
        part_core(b, 0).wait_recv()
        result = acc[b] + precv[b, 0].astype(jnp.float32)
        for j in range(1, ny):
            part_y(b, j).wait_recv()
            result += yrecv[b, j - 1].astype(jnp.float32)
        out_ref[pl.ds(pl.multiple_of(b * BLOCK_TOKENS, BLOCK_TOKENS), BLOCK_TOKENS)] = (
            result.astype(jnp.bfloat16)
        )
        for j in range(1, ny):
            tok_y(b, j).wait_send()
            tok_fwd(b, j).wait_send()
            part_y(b, j).wait_send()
        for j in range(ny):
            part_core(b, j).wait_send()
        return carry

    lax.fori_loop(0, blocks, finish, 0)
    tok_core().wait_send()
    own_z(lambda copy: copy.wait_send())
    along_z(range(1, nz), lambda source, way: None, lambda copy: copy.wait_send())
    for source in range(nz):
        for i in range(1, nx):
            kv_x(source, i, True).wait_send()


def local(
    n_seq,
    n_head,
    tokens,
    norm_gain,
    w_query,
    key_weight,
    value_weight,
    w_out,
    ancestor_blocks,
    visible_counts,
):
    rows, width = tokens.shape
    blocks = rows // BLOCK_TOKENS
    q_cols = w_query.shape[1]
    kv_cols = key_weight.shape[1]
    ny = n_head // 2
    nx = ny
    nz = n_seq // nx
    half = HEAD_SIZE // 2
    frequency = ROPE_BASE ** (-(np.arange(half) * 2.0) / HEAD_SIZE)
    frequency = np.concatenate([frequency, frequency]).astype(np.float32)[None]
    dma = pltpu.SemaphoreType.DMA
    vmem = pl.BlockSpec(memory_space=pltpu.VMEM)
    smem = pl.BlockSpec(memory_space=pltpu.SMEM)
    hbm = pl.BlockSpec(memory_space=pl.ANY)
    bf16, f32 = jnp.bfloat16, jnp.float32
    return pl.pallas_call(
        functools.partial(kernel, n_seq, n_head),
        out_shape=jax.ShapeDtypeStruct((rows, width), bf16),
        in_specs=[hbm, vmem, vmem, hbm, hbm, hbm, hbm, smem, smem],
        out_specs=vmem,
        scratch_shapes=[
            pltpu.VMEM((ny, 2, rows, width), bf16),
            pltpu.VMEM((ny, 2 * width, q_cols), bf16),
            pltpu.VMEM((ny, 2 * width, kv_cols), bf16),
            pltpu.VMEM((ny, 2 * width, kv_cols), bf16),
            pltpu.VMEM(w_out.shape, bf16),
            pltpu.VMEM((rows, 2 * width), bf16),
            pltpu.VMEM((BLOCK_TOKENS, (ny - 1) * 2 * width), bf16),
            pltpu.VMEM((rows, q_cols + 2 * kv_cols), f32),
            pltpu.VMEM((blocks, BLOCK_TOKENS, HEAD_SIZE), f32),
            pltpu.VMEM((blocks, BLOCK_TOKENS, HEAD_SIZE), f32),
            pltpu.VMEM((blocks, BLOCK_TOKENS, HEAD_SIZE), f32),
            pltpu.VMEM((blocks, q_cols // HEAD_SIZE, BLOCK_TOKENS, 2 * HEAD_SIZE), bf16),
            pltpu.VMEM((n_seq + blocks, BLOCK_TOKENS, 2 * kv_cols), bf16),
            pltpu.VMEM((kv_cols // HEAD_SIZE, 2 * HEAD_SIZE, KEYS), bf16),
            pltpu.VMEM((kv_cols // HEAD_SIZE, KEYS, 2 * HEAD_SIZE), bf16),
            pltpu.VMEM((BLOCK_TOKENS, q_cols), bf16),
            pltpu.VMEM((blocks, ny, BLOCK_TOKENS, width), bf16),
            pltpu.VMEM((blocks, ny, BLOCK_TOKENS, width), bf16),
            pltpu.VMEM((ny - 1, BLOCK_TOKENS, width), f32),
            pltpu.VMEM((blocks, BLOCK_TOKENS, width), f32),
            pltpu.VMEM((blocks, ny - 1, BLOCK_TOKENS, width), bf16),
            pltpu.VMEM((blocks, ny - 1, BLOCK_TOKENS, width), bf16),
            dma((3, ny)),
            dma,
            dma,
            dma((blocks, ny - 1)),
            dma((blocks, ny - 1)),
            dma,
            dma,
            dma((blocks, ny - 1)),
            dma((blocks, ny - 1)),
            dma((nz + 2,)),
            dma((nz,)),
            dma((nz, nx - 1)),
            dma((nz, nx - 1)),
            dma((blocks, ny)),
            dma((blocks, ny)),
            dma((blocks, ny - 1)),
            dma((blocks, ny - 1)),
        ],
        compiler_params=pltpu.CompilerParams(
            collective_id=0, has_side_effects=True, vmem_limit_bytes=60 * 1024 * 1024
        ),
        cost_estimate=pl.CostEstimate(
            flops=13 * 10**9, bytes_accessed=25 * 10**6, transcendentals=5 * 10**6
        ),
    )(
        tokens,
        norm_gain[None],
        jnp.asarray(frequency),
        w_query,
        key_weight,
        value_weight,
        w_out,
        ancestor_blocks,
        visible_counts,
    )


def solution(mesh):
    placed = (
        P("seq", "head"),
        P(),
        P(None, "head"),
        P(None, "head"),
        P(None, "head"),
        P("head", None),
        P("seq", None),
        P("seq", None),
    )
    return jax.shard_map(
        functools.partial(local, mesh.shape["seq"], mesh.shape["head"]),
        mesh=mesh,
        in_specs=placed,
        out_specs=P("seq", "head"),
        check_vma=False,
    )
```
